32 devices in a mesh: ctx: 8 (over z, x), tp: 4 (over y, core).
Axes of the slice: x: 2, y: 2, z: 4, core: 2. Of those that a mesh axis runs over, the one named last changes fastest.
Arguments:
- tokens: bfloat16 [1024, 4096], P('ctx', 'tp'), may hold values from -6 to 6
- routes: int32 [1024, 8], P('ctx'), may hold values from 0 to 127, all different within a row
- gates: float32 [1024, 8], P('ctx'), may hold values from 0.1 to 1
- w_gate: bfloat16 [8, 4096, 1536], P('ctx', None, 'tp'), may hold values from -0.09375 to 0.09375
- w_up: bfloat16 [8, 4096, 1536], P('ctx', None, 'tp'), may hold values from -0.09375 to 0.09375
- w_down: bfloat16 [8, 1536, 4096], P('ctx', 'tp'), may hold values from -0.15625 to 0.15625
- d_out: bfloat16 [1024, 4096], P('ctx', 'tp'), may hold values from -6 to 6
Outputs:
- mixed: bfloat16 [1024, 4096], P('ctx', 'tp')
- d_tokens: bfloat16 [1024, 4096], P('ctx', 'tp')
- d_gates: float32 [1024, 8], P('ctx')
- d_w_gate: bfloat16 [8, 4096, 1536], P('ctx', None, 'tp')
- d_w_up: bfloat16 [8, 4096, 1536], P('ctx', None, 'tp')
- d_w_down: bfloat16 [8, 1536, 4096], P('ctx', 'tp')
The draws below stay inside these ranges and needn't reach their ends.
Inputs may be any that keep to these rules, and one draw needn't show every extreme that they name: `routes`: each row names 8 different experts of 128; pairs naming an expert of 8 or above are outside this window.
All inputs are finite; a program needn't handle non-finite values.
Results may differ from the reference program's by a relative error of at most 0.0063.
Values may be sent and summed in bfloat16 or wider, within the bound.
No kernel may reach another device: no remote copies, remote signals or barrier semaphores. Data moves between devices by JAX's collectives and lax.ppermute only.
A program may use at most 128 MiB of HBM per device.

```python
import jax
import jax.numpy as jnp
from jax import lax

D = 4096
FF = 1536
EXPERTS_ALL = 128
TOPK = 8
TOK_DEV = 128
EXPERTS = 8
CAP = 16
TOKENS = 1024


def levels(key, dims, split, low, high):
    factor_of, own = 1.0, jax.random.fold_in(key, 6)
    for dim, blocks in split:
        steps = jnp.exp(jax.random.uniform(jax.random.fold_in(own, dim), (blocks,), jnp.float32, low / len(split), high / len(split)))
        factor_of = factor_of * jnp.repeat(steps, dims[dim] // blocks).reshape([-1 if axis == dim else 1 for axis in range(len(dims))])
    return factor_of


def picks_of(key, rows, count, top, lift):
    ranking = jax.random.permutation(jax.random.fold_in(key, 1), count)
    boost = ranking
    for power in range(3):
        boost = boost * boost // count
    boost = boost * lift // count
    lots = jax.random.randint(jax.random.fold_in(key, 2), (rows, count), 0, 4096) + boost
    holders = jax.random.permutation(jax.random.fold_in(key, 3), rows)[jnp.arange(count) % rows]
    lots = jnp.where(jnp.arange(rows)[:, None] == holders[None, :], 1 << 14, lots)
    score = lots * count + jnp.arange(count)
    return lax.top_k(score.astype(jnp.int32), top)[1].astype(jnp.int32)


def bell_draw(rng, shape, spread, most, cuts=(), kind=jnp.bfloat16):
    values = jax.random.normal(rng, shape, jnp.float32) * spread
    if len(cuts) > 0:
        values = levels(rng, shape, cuts, -0.22, 0.18) * values
    return jnp.clip(values, min=-most, max=most).astype(kind)


def setup_inputs(seed: int = 0) -> dict:
    keys = jax.random.split(jax.random.key(seed), 8)
    return {
        "tokens": bell_draw(keys[0], (TOKENS, D), 1.0, 6.0, ((0, 8), (1, 4))),
        "routes": picks_of(keys[1], TOKENS, EXPERTS_ALL, TOPK, 512),
        "gates": jnp.clip(0.1 + 0.9 * jax.random.uniform(keys[2], (TOKENS, TOPK), jnp.float32) ** levels(keys[2], (TOKENS, TOPK), ((0, 8),), -0.2, 0.2), 0.1, 1.0),
        "w_gate": bell_draw(keys[3], (EXPERTS, D, FF), D ** -0.5, 0.09375, ((0, 8), (2, 4))),
        "w_up": bell_draw(keys[4], (EXPERTS, D, FF), D ** -0.5, 0.09375, ((0, 8), (2, 4))),
        "w_down": bell_draw(keys[5], (EXPERTS, FF, D), FF ** -0.5, 0.15625, ((0, 8), (1, 4))),
        "d_out": bell_draw(keys[6], (TOKENS, D), 1.0, 6.0, ((0, 8), (1, 4))),
    }


def expert_pass(items):
    xrow, drow, wg, wu, wd = items
    act = jnp.dot(xrow, wg, preferred_element_type=jnp.float32)
    lin = jnp.dot(xrow, wu, preferred_element_type=jnp.float32)
    sig = jax.nn.sigmoid(act)
    hidden = (act * sig * lin).astype(jnp.bfloat16)
    eout = jnp.dot(hidden, wd, preferred_element_type=jnp.float32).astype(jnp.bfloat16)
    dhid = jnp.dot(drow, wd.T, preferred_element_type=jnp.float32)
    grad_down = jnp.dot(hidden.T, drow, preferred_element_type=jnp.float32).astype(jnp.bfloat16)
    dlin = (dhid * act * sig).astype(jnp.bfloat16)
    dact = (dhid * lin * sig * (1.0 + act * (1.0 - sig))).astype(jnp.bfloat16)
    grad_gate = jnp.dot(xrow.T, dact, preferred_element_type=jnp.float32).astype(jnp.bfloat16)
    grad_up = jnp.dot(xrow.T, dlin, preferred_element_type=jnp.float32).astype(jnp.bfloat16)
    dxin = (jnp.dot(dact, wg.T, preferred_element_type=jnp.float32)
            + jnp.dot(dlin, wu.T, preferred_element_type=jnp.float32)).astype(jnp.bfloat16)
    return eout, dxin, grad_gate, grad_up, grad_down


def reference(tokens, routes, gates, w_gate, w_up, w_down, d_out):
    blocks = TOKENS // TOK_DEV
    flat = routes.reshape(blocks, TOK_DEV * TOPK)
    onehot = (flat[:, :, None] == jnp.arange(EXPERTS, dtype=jnp.int32)[None, None, :]).astype(jnp.int32)
    before = jnp.sum((jnp.cumsum(onehot, axis=1) - onehot) * onehot, axis=-1)
    keep = (flat < EXPERTS) & (before < CAP)
    source = jnp.arange(blocks, dtype=jnp.int32)[:, None]
    erow = jnp.where(keep, flat, EXPERTS).reshape(-1).astype(jnp.int32)
    prow = jnp.where(keep, source * CAP + before, 0).reshape(-1).astype(jnp.int32)
    keepf = keep.reshape(-1).astype(jnp.float32)
    owner = jnp.repeat(jnp.arange(TOKENS, dtype=jnp.int32), TOPK)
    weight = gates.reshape(-1)
    rows = blocks * CAP
    xin = jnp.zeros((EXPERTS, rows, D), jnp.bfloat16).at[erow, prow].set(tokens[owner], mode="drop")
    scaled = (weight[:, None] * d_out[owner].astype(jnp.float32)).astype(jnp.bfloat16)
    dyin = jnp.zeros((EXPERTS, rows, D), jnp.bfloat16).at[erow, prow].set(scaled, mode="drop")
    eout, dxin, grad_gate, grad_up, grad_down = lax.map(expert_pass, (xin, dyin, w_gate, w_up, w_down))
    eclip = jnp.minimum(erow, EXPERTS - 1)
    picked = eout[eclip, prow].astype(jnp.float32) * keepf[:, None]
    mixed = jnp.sum(((weight * keepf)[:, None] * picked).reshape(TOKENS, TOPK, D), axis=1).astype(jnp.bfloat16)
    dpick = dxin[eclip, prow].astype(jnp.float32) * keepf[:, None]
    d_tokens = jnp.sum(dpick.reshape(TOKENS, TOPK, D), axis=1).astype(jnp.bfloat16)
    d_gates = jnp.sum(d_out[owner].astype(jnp.float32) * picked, axis=-1).reshape(TOKENS, TOPK)
    return mixed, d_tokens, d_gates, grad_gate, grad_up, grad_down
```

```python
import jax
import jax.numpy as jnp
from jax import lax
from jax.experimental import pallas as pl
from jax.experimental.pallas import tpu as pltpu
from jax.sharding import PartitionSpec as P

CAP = 16
F32 = jnp.float32
BF16 = jnp.bfloat16
VMEM_BYTES = 40 * 1024 * 1024
NN = (((1,), (0,)), ((), ()))
NT = (((1,), (1,)), ((), ()))
TN = (((0,), (0,)), ((), ()))


def dot(a, b, dims=NN):
    return lax.dot_general(a, b, dims, preferred_element_type=F32)


def params():
    return pltpu.CompilerParams(vmem_limit_bytes=VMEM_BYTES)


def cost(flops, nbytes):
    return pl.CostEstimate(flops=flops, bytes_accessed=nbytes, transcendentals=0)


def vspec():
    return pl.BlockSpec(memory_space=pltpu.VMEM)


def aspec():
    return pl.BlockSpec(memory_space=pl.ANY)


def dispatch_kernel(routes, gates, tokens, d_out, xs, ds, sel, pick, w_hi, w_lo):
    experts, cap, quarter = xs.shape
    topk, tok = routes.shape
    slots = experts * cap
    r = routes[...]
    match = r[None] == lax.broadcasted_iota(jnp.int32, (experts, topk, tok), 0)
    hit = jnp.sum(jnp.where(match, 1.0, 0.0), axis=1)
    gate = jnp.sum(jnp.where(match, gates[...][None], 0.0), axis=1)
    earlier = lax.broadcasted_iota(jnp.int32, (tok, tok), 0) < lax.broadcasted_iota(
        jnp.int32, (tok, tok), 1
    )
    before = dot(hit.astype(BF16), jnp.where(earlier, 1.0, 0.0).astype(BF16))
    place = jnp.where(hit > 0.0, before, -1.0)[:, None, :]
    row = lax.broadcasted_iota(jnp.int32, (experts, cap, tok), 1).astype(F32)
    chosen = jnp.where(place == row, 1.0, 0.0)
    weight = (chosen * gate[:, None, :]).reshape(slots, tok)
    chosen = chosen.reshape(slots, tok)
    select = chosen.astype(BF16)
    xs[...] = dot(select, tokens[...]).astype(BF16).reshape(experts, cap, quarter)
    slot_gate = jnp.sum(weight, axis=1, keepdims=True)
    ds[...] = (slot_gate * dot(select, d_out[...])).astype(BF16).reshape(experts, cap, quarter)
    sel[...] = select
    pick[...] = chosen.T.astype(BF16)
    back = weight.T
    high = back.astype(BF16)
    w_hi[...] = high
    w_lo[...] = (back - high.astype(F32)).astype(BF16)


def dispatch(routes_t, gates_t, tokens, d_out, experts):
    tok, quarter = tokens.shape
    slots = experts * CAP
    return pl.pallas_call(
        dispatch_kernel,
        out_shape=(
            jax.ShapeDtypeStruct((experts, CAP, quarter), BF16),
            jax.ShapeDtypeStruct((experts, CAP, quarter), BF16),
            jax.ShapeDtypeStruct((slots, tok), BF16),
            jax.ShapeDtypeStruct((tok, slots), BF16),
            jax.ShapeDtypeStruct((tok, slots), BF16),
            jax.ShapeDtypeStruct((tok, slots), BF16),
        ),
        in_specs=[vspec()] * 4,
        out_specs=(vspec(),) * 6,
        compiler_params=params(),
        cost_estimate=cost(4 * slots * tok * quarter, 8 * tok * quarter),
        name="dispatch",
    )(routes_t, gates_t, tokens, d_out)


ORDER = (0, 1, 2, 3)


def quarter_of(me, flip, size):
    return pl.ds(pl.multiple_of((me ^ flip) * size, size), size)


def fetch(src, dst, sem, part):
    copy = pltpu.make_async_copy(src.at[part], dst.at[part], sem)
    copy.start()
    return copy


def forward_kernel(
    x0, x1, x2, x3, wg, wu, wd, act, lin, hidden, send, keep, vg, vu, vd, sem
):
    me = lax.axis_index("tp")
    size = x0.shape[1]
    xs = (x0, x1, x2, x3)
    loads = []
    for i in ORDER:
        part = (quarter_of(me, i, size), slice(None))
        loads.append((fetch(wg, vg, sem.at[0, i], part), fetch(wu, vu, sem.at[1, i], part)))
    tail = [
        fetch(wd, vd, sem.at[2, i], (slice(None), quarter_of(me, i, size))) for i in (3, 1, 2, 0)
    ]
    a = b = None
    for i in ORDER:
        part = quarter_of(me, i, size)
        x = xs[i][...]
        loads[i][0].wait()
        pa = dot(x, vg[part, :])
        loads[i][1].wait()
        pb = dot(x, vu[part, :])
        a = pa if a is None else a + pa
        b = pb if b is None else b + pb
    act[...] = a
    lin[...] = b
    h = (a * jax.nn.sigmoid(a) * b).astype(BF16)
    hidden[...] = h
    for n, i in enumerate((3, 1, 2, 0)):
        tail[n].wait()
        p = dot(h, vd[:, quarter_of(me, i, size)])
        if n < 2:
            send[n] = p.astype(BF16)
        else:
            keep[n - 2] = p


def forward(xs, wg, wu, wd):
    rows, size = xs[0].shape
    d, ff = wg.shape
    return pl.pallas_call(
        forward_kernel,
        out_shape=(
            jax.ShapeDtypeStruct((rows, ff), F32),
            jax.ShapeDtypeStruct((rows, ff), F32),
            jax.ShapeDtypeStruct((rows, ff), BF16),
            jax.ShapeDtypeStruct((2, rows, size), BF16),
            jax.ShapeDtypeStruct((2, rows, size), F32),
        ),
        in_specs=[vspec()] * 4 + [aspec()] * 3,
        out_specs=(vspec(),) * 5,
        scratch_shapes=[
            pltpu.VMEM((d, ff), BF16),
            pltpu.VMEM((d, ff), BF16),
            pltpu.VMEM((ff, d), BF16),
            pltpu.SemaphoreType.DMA((3, 4)),
        ],
        compiler_params=params(),
        cost_estimate=cost(6 * rows * d * ff, 6 * d * ff + 6 * rows * d),
        name="forward",
    )(*xs, wg, wu, wd)


def backward_kernel(
    d0, d1, d2, d3, act, lin, wg, wu, wd, dact, dlin, send, keep, vg, vu, vd, sem
):
    me = lax.axis_index("tp")
    size = d0.shape[1]
    ds = (d0, d1, d2, d3)
    head = [
        fetch(wd, vd, sem.at[2, i], (slice(None), quarter_of(me, i, size))) for i in ORDER
    ]
    loads = []
    for i in (3, 1, 2, 0):
        part = (quarter_of(me, i, size), slice(None))
        loads.append((fetch(wg, vg, sem.at[0, i], part), fetch(wu, vu, sem.at[1, i], part)))
    dhid = None
    for i in ORDER:
        head[i].wait()
        p = dot(ds[i][...], vd[:, quarter_of(me, i, size)], NT)
        dhid = p if dhid is None else dhid + p
    a = act[...]
    s = jax.nn.sigmoid(a)
    dl = (dhid * (a * s)).astype(BF16)
    da = (dhid * lin[...] * s * (1.0 + a * (1.0 - s))).astype(BF16)
    dlin[...] = dl
    dact[...] = da
    for n, i in enumerate((3, 1, 2, 0)):
        part = quarter_of(me, i, size)
        loads[n][0].wait()
        loads[n][1].wait()
        p = dot(da, vg[part, :], NT) + dot(dl, vu[part, :], NT)
        if n < 2:
            send[n] = p.astype(BF16)
        else:
            keep[n - 2] = p


def backward(ds, act, lin, wg, wu, wd):
    rows, size = ds[0].shape
    d, ff = wg.shape
    return pl.pallas_call(
        backward_kernel,
        out_shape=(
            jax.ShapeDtypeStruct((rows, ff), BF16),
            jax.ShapeDtypeStruct((rows, ff), BF16),
            jax.ShapeDtypeStruct((2, rows, size), BF16),
            jax.ShapeDtypeStruct((2, rows, size), F32),
        ),
        in_specs=[vspec()] * 6 + [aspec()] * 3,
        out_specs=(vspec(),) * 4,
        scratch_shapes=[
            pltpu.VMEM((d, ff), BF16),
            pltpu.VMEM((d, ff), BF16),
            pltpu.VMEM((ff, d), BF16),
            pltpu.SemaphoreType.DMA((3, 4)),
        ],
        compiler_params=params(),
        cost_estimate=cost(6 * rows * d * ff, 6 * d * ff + 6 * rows * d),
        name="backward",
    )(*ds, act, lin, wg, wu, wd)


def grads_kernel(
    x0, x1, x2, x3, d0, d1, d2, d3, hidden, dact, dlin, gg, gu, gd, vg, vu, vd, sem
):
    me = lax.axis_index("tp")
    size = x0.shape[1]
    xs, ds = (x0, x1, x2, x3), (d0, d1, d2, d3)
    h = hidden[...]
    da = dact[...]
    dl = dlin[...]
    stores = []
    for i in ORDER:
        part = quarter_of(me, i, size)
        rows = (part, slice(None))
        cols = (slice(None), part)
        x = xs[i][...]
        vg[part, :] = dot(x, da, TN).astype(BF16)
        stores.append(fetch(vg, gg, sem.at[0, i], rows))
        vu[part, :] = dot(x, dl, TN).astype(BF16)
        stores.append(fetch(vu, gu, sem.at[1, i], rows))
        vd[:, part] = dot(h, ds[i][...], TN).astype(BF16)
        stores.append(fetch(vd, gd, sem.at[2, i], cols))
    for store in stores:
        store.wait()


def grads(xs, ds, hidden, dact, dlin):
    rows, size = xs[0].shape
    ff = hidden.shape[1]
    d = 4 * size
    return pl.pallas_call(
        grads_kernel,
        out_shape=(
            jax.ShapeDtypeStruct((d, ff), BF16),
            jax.ShapeDtypeStruct((d, ff), BF16),
            jax.ShapeDtypeStruct((ff, d), BF16),
        ),
        in_specs=[vspec()] * 11,
        out_specs=(aspec(),) * 3,
        scratch_shapes=[
            pltpu.VMEM((d, ff), BF16),
            pltpu.VMEM((d, ff), BF16),
            pltpu.VMEM((ff, d), BF16),
            pltpu.SemaphoreType.DMA((3, 4)),
        ],
        compiler_params=params(),
        cost_estimate=cost(6 * rows * d * ff, 6 * d * ff + 4 * rows * d),
        name="grads",
    )(*xs, *ds, hidden, dact, dlin)


def mix_kernel(back, w_hi, w_lo, sel, d_out, routes, mixed, dots):
    slots, tok = sel.shape
    topk = routes.shape[0]
    experts = slots // CAP
    o = back[...]
    mixed[...] = (dot(w_hi[...], o) + dot(w_lo[...], o)).astype(BF16)
    select = sel[...]
    per_slot = jnp.sum(dot(select, d_out[...]) * o.astype(F32), axis=1, keepdims=True)
    spread = select.astype(F32) * per_slot
    per_expert = jnp.sum(spread.reshape(experts, CAP, tok), axis=1)
    match = routes[...][None] == lax.broadcasted_iota(jnp.int32, (experts, topk, tok), 0)
    dots[...] = jnp.sum(jnp.where(match, per_expert[:, None, :], 0.0), axis=0)


def mix(back, w_hi, w_lo, sel, d_out, routes_t):
    slots, quarter = back.shape
    topk, tok = routes_t.shape
    return pl.pallas_call(
        mix_kernel,
        out_shape=(
            jax.ShapeDtypeStruct((tok, quarter), BF16),
            jax.ShapeDtypeStruct((topk, tok), F32),
        ),
        in_specs=[vspec()] * 6,
        out_specs=(vspec(),) * 2,
        compiler_params=params(),
        cost_estimate=cost(6 * slots * tok * quarter, 6 * tok * quarter),
        name="mix",
    )(back, w_hi, w_lo, sel, d_out, routes_t)


def collect_kernel(back, pick, d_tokens):
    d_tokens[...] = dot(pick[...], back[...]).astype(BF16)


def collect(back, pick):
    slots, quarter = back.shape
    tok = pick.shape[0]
    return pl.pallas_call(
        collect_kernel,
        out_shape=jax.ShapeDtypeStruct((tok, quarter), BF16),
        in_specs=[vspec()] * 2,
        out_specs=vspec(),
        compiler_params=params(),
        cost_estimate=cost(2 * slots * tok * quarter, 4 * tok * quarter),
        name="collect",
    )(back, pick)


def swap(x, flip):
    return lax.ppermute(x, "tp", [(i, i ^ flip) for i in range(4)])


def exchange(x):
    return lax.all_to_all(x, "ctx", split_axis=0, concat_axis=0, tiled=True)


def gather(own):
    near = swap(own, 1)
    far = swap(own, 2)
    return (own, near, far, swap(far, 1))


def scatter_sum(send, keep):
    got = swap(send, 1)
    across = swap((keep[0] + got[0].astype(F32)).astype(BF16), 2)
    return (keep[1] + got[1].astype(F32) + across.astype(F32)).astype(BF16)


def on_device(tokens, routes, gates, w_gate, w_up, w_down, d_out):
    tok, quarter = tokens.shape
    sources = lax.axis_size("ctx")
    experts = sources * w_gate.shape[0]
    slots = experts * CAP
    rows = sources * CAP
    wg, wu, wd = w_gate[0], w_up[0], w_down[0]
    routes_t = routes.T
    xs, ds, sel, pick, w_hi, w_lo = dispatch(routes_t, gates.T, tokens, d_out, experts)
    xq = gather(exchange(xs).reshape(rows, quarter))
    dq = gather(exchange(ds).reshape(rows, quarter))
    act, lin, hidden, send_out, keep_out = forward(xq, wg, wu, wd)
    dact, dlin, send_dx, keep_dx = backward(dq, act, lin, wg, wu, wd)
    out_rows = scatter_sum(send_out, keep_out)
    back_out = exchange(out_rows.reshape(sources, CAP, quarter)).reshape(slots, quarter)
    dx_rows = scatter_sum(send_dx, keep_dx)
    back_dx = exchange(dx_rows.reshape(sources, CAP, quarter)).reshape(slots, quarter)
    grad_gate, grad_up, grad_down = grads(xq, dq, hidden, dact, dlin)
    mixed, dots = mix(back_out, w_hi, w_lo, sel, d_out, routes_t)
    dots = dots + swap(dots, 1)
    dots = dots + swap(dots, 2)
    d_tokens = collect(back_dx, pick)
    return (mixed, d_tokens, dots.T, grad_gate[None], grad_up[None], grad_down[None])


def solution(mesh):
    placed = (
        P("ctx", "tp"),
        P("ctx", None),
        P("ctx", None),
        P("ctx", None, "tp"),
        P("ctx", None, "tp"),
        P("ctx", "tp", None),
        P("ctx", "tp"),
    )
    return jax.shard_map(
        on_device,
        mesh=mesh,
        in_specs=placed,
        out_specs=(
            P("ctx", "tp"),
            P("ctx", "tp"),
            P("ctx", None),
            P("ctx", None, "tp"),
            P("ctx", None, "tp"),
            P("ctx", "tp", None),
        ),
        check_vma=False,
    )
```

```python
import functools

import jax
import jax.numpy as jnp
from jax import lax
from jax.experimental import pallas as pl
from jax.experimental.pallas import tpu as pltpu
from jax.sharding import PartitionSpec as P

CAP = 16
F32 = jnp.float32
BF16 = jnp.bfloat16
NN = (((1,), (0,)), ((), ()))
NT = (((1,), (1,)), ((), ()))
TN = (((0,), (0,)), ((), ()))


def dot(a, b, dims=NN):
    return lax.dot_general(a, b, dims, preferred_element_type=F32)


def params(mib=16):
    return pltpu.CompilerParams(vmem_limit_bytes=mib * 1024 * 1024)


def cost(flops, nbytes):
    return pl.CostEstimate(flops=flops, bytes_accessed=nbytes, transcendentals=0)


def vspec():
    return pl.BlockSpec(memory_space=pltpu.VMEM)


def hspec():
    return pl.BlockSpec(memory_space=pltpu.HBM)


def aspec():
    return pl.BlockSpec(memory_space=pl.ANY)


def fixed(x):
    return pltpu.with_memory_space_constraint(x, pltpu.HBM)


def dispatch_kernel(
    routes_in, gates_in, tokens_in, d_in, slots_out, sel, pick, w_hi, w_lo, routes, gates, tokens, d_out, sem
):
    experts, cap2, quarter = slots_out.shape
    cap = cap2 // 2
    topk, tok = routes.shape
    slots = experts * cap
    loads = [
        pltpu.make_async_copy(src, dst, sem.at[i])
        for i, (src, dst) in enumerate(
            ((routes_in, routes), (gates_in, gates), (tokens_in, tokens), (d_in, d_out))
        )
    ]
    for load in loads:
        load.start()
    loads[0].wait()
    loads[1].wait()
    match = routes[...][None] == lax.broadcasted_iota(jnp.int32, (experts, topk, tok), 0)
    hit = jnp.sum(jnp.where(match, 1.0, 0.0), axis=1)
    gate = jnp.sum(jnp.where(match, gates[...][None], 0.0), axis=1)
    earlier = lax.broadcasted_iota(jnp.int32, (tok, tok), 0) < lax.broadcasted_iota(
        jnp.int32, (tok, tok), 1
    )
    before = dot(hit.astype(BF16), jnp.where(earlier, 1.0, 0.0).astype(BF16))
    place = jnp.where(hit > 0.0, before, -1.0)[:, None, :]
    row = lax.broadcasted_iota(jnp.int32, (experts, cap, tok), 1).astype(F32)
    chosen = jnp.where(place == row, 1.0, 0.0)
    weight = (chosen * gate[:, None, :]).reshape(slots, tok)
    chosen = chosen.reshape(slots, tok)
    select = chosen.astype(BF16)
    loads[2].wait()
    x = dot(select, tokens[...]).astype(BF16)
    slots_out[:, :cap, :] = x.reshape(experts, cap, quarter)
    slot_gate = jnp.sum(weight, axis=1, keepdims=True)
    loads[3].wait()
    d = (slot_gate * dot(select, d_out[...])).astype(BF16)
    slots_out[:, cap:, :] = d.reshape(experts, cap, quarter)
    sel[...] = select
    pick[...] = chosen.T.astype(BF16)
    back = weight.T
    high = back.astype(BF16)
    w_hi[...] = high
    w_lo[...] = (back - high.astype(F32)).astype(BF16)


def dispatch(routes_t, gates_t, tokens, d_out, experts):
    tok, quarter = tokens.shape
    slots = experts * CAP
    return pl.pallas_call(
        dispatch_kernel,
        out_shape=(
            jax.ShapeDtypeStruct((experts, 2 * CAP, quarter), BF16),
            jax.ShapeDtypeStruct((slots, tok), BF16),
            jax.ShapeDtypeStruct((tok, slots), BF16),
            jax.ShapeDtypeStruct((tok, slots), BF16),
            jax.ShapeDtypeStruct((tok, slots), BF16),
        ),
        in_specs=[hspec()] * 4,
        out_specs=(vspec(),) * 5,
        scratch_shapes=[
            pltpu.VMEM(routes_t.shape, jnp.int32),
            pltpu.VMEM(gates_t.shape, F32),
            pltpu.VMEM(tokens.shape, BF16),
            pltpu.VMEM(d_out.shape, BF16),
            pltpu.SemaphoreType.DMA((4,)),
        ],
        compiler_params=params(),
        cost_estimate=cost(4 * slots * tok * quarter, 8 * tok * quarter),
        name="dispatch",
    )(*(fixed(v) for v in (routes_t, gates_t, tokens, d_out)))


def quarter_of(me, flip, size):
    return pl.ds(pl.multiple_of((me ^ flip) * size, size), size)


def fetch(src, dst, sem, part):
    copy = pltpu.make_async_copy(src.at[part], dst.at[part], sem)
    copy.start()
    return copy


def forward_kernel(
    x0, x1, x2, x3, wg, wu, wd, act, lin, hidden, vg, vu, vd, send_far, send_near, keep_far, keep_own, sem
):
    me = lax.axis_index("tp")
    size = x0.shape[1]
    xs = (x0, x1, x2, x3)
    loads, last = [], []
    for i in range(4):
        part = (quarter_of(me, i, size), slice(None))
        loads.append((fetch(wg, vg, sem.at[0, i], part), fetch(wu, vu, sem.at[1, i], part)))
    for n, i in enumerate((3, 2, 1, 0)):
        last.append(fetch(wd, vd, sem.at[2, n], (slice(None), quarter_of(me, i, size))))
    a = b = None
    for i in range(4):
        part = quarter_of(me, i, size)
        x = xs[i][...]
        loads[i][0].wait()
        pa = dot(x, vg[part, :])
        loads[i][1].wait()
        pb = dot(x, vu[part, :])
        a = pa if a is None else a + pa
        b = pb if b is None else b + pb
    act[...] = a
    lin[...] = b
    h = (a * jax.nn.sigmoid(a) * b).astype(BF16)
    hidden[...] = h
    for n, (i, out) in enumerate(((3, send_far), (2, keep_far), (1, send_near), (0, keep_own))):
        last[n].wait()
        out[...] = dot(h, vd[:, quarter_of(me, i, size)]).astype(out.dtype)


def forward(xs, wg, wu, wd):
    rows, size = xs[0].shape
    d, ff = wg.shape
    return pl.pallas_call(
        forward_kernel,
        out_shape=(
            jax.ShapeDtypeStruct((rows, ff), F32),
            jax.ShapeDtypeStruct((rows, ff), F32),
            jax.ShapeDtypeStruct((rows, ff), BF16),
            jax.ShapeDtypeStruct((d, ff), BF16),
            jax.ShapeDtypeStruct((d, ff), BF16),
            jax.ShapeDtypeStruct((ff, d), BF16),
            jax.ShapeDtypeStruct((rows, size), BF16),
            jax.ShapeDtypeStruct((rows, size), BF16),
            jax.ShapeDtypeStruct((rows, size), F32),
            jax.ShapeDtypeStruct((rows, size), F32),
        ),
        in_specs=[vspec()] * 4 + [hspec()] * 3,
        out_specs=(vspec(),) * 10,
        scratch_shapes=[pltpu.SemaphoreType.DMA((3, 4))],
        compiler_params=params(),
        cost_estimate=cost(6 * rows * d * ff, 6 * d * ff + 6 * rows * d),
        name="forward",
    )(*xs, fixed(wg), fixed(wu), fixed(wd))


def hidden_grad_kernel(d0, d1, d2, d3, act, lin, vd, dact, dlin):
    me = lax.axis_index("tp")
    size = d0.shape[1]
    ds = (d0, d1, d2, d3)
    dhid = None
    for i in range(4):
        p = dot(ds[i][...], vd[:, quarter_of(me, i, size)], NT)
        dhid = p if dhid is None else dhid + p
    a = act[...]
    s = jax.nn.sigmoid(a)
    dlin[...] = (dhid * (a * s)).astype(BF16)
    dact[...] = (dhid * lin[...] * s * (1.0 + a * (1.0 - s))).astype(BF16)


def hidden_grad(ds, act, lin, vd):
    rows, size = ds[0].shape
    ff, d = vd.shape
    return pl.pallas_call(
        hidden_grad_kernel,
        out_shape=(
            jax.ShapeDtypeStruct((rows, ff), BF16),
            jax.ShapeDtypeStruct((rows, ff), BF16),
        ),
        in_specs=[vspec()] * 7,
        out_specs=(vspec(),) * 2,
        compiler_params=params(),
        cost_estimate=cost(2 * rows * d * ff, 2 * d * ff + 2 * rows * d),
        name="hidden_grad",
    )(*ds, act, lin, vd)


def input_grad_kernel(flips, after, dact, dlin, vg, vu, send, keep):
    me = lax.axis_index("tp")
    size = send.shape[1]
    da = dact[...]
    dl = dlin[...]
    for i, out in zip(flips, (send, keep)):
        part = quarter_of(me, i, size)
        p = dot(da, vg[part, :], NT) + dot(dl, vu[part, :], NT)
        out[...] = p.astype(out.dtype)


def input_grad(flips, after, dact, dlin, vg, vu):
    rows, ff = dact.shape
    d = vg.shape[0]
    return pl.pallas_call(
        functools.partial(input_grad_kernel, flips),
        out_shape=(
            jax.ShapeDtypeStruct((rows, d // 4), BF16),
            jax.ShapeDtypeStruct((rows, d // 4), F32),
        ),
        in_specs=[aspec()] + [vspec()] * 4,
        out_specs=(vspec(),) * 2,
        compiler_params=params(),
        cost_estimate=cost(2 * rows * d * ff, 2 * d * ff + 3 * rows * d),
        name="input_grad",
    )(after, dact, dlin, vg, vu)


def grads_kernel(*refs):
    given, (gg, gu, gd), held, (vg, vu, vd, sem, load_sem) = (
        refs[:11],
        refs[11:14],
        refs[14:25],
        refs[25:],
    )
    me = lax.axis_index("tp")
    size = given[0].shape[1]
    loads = [
        pltpu.make_async_copy(src, dst, load_sem.at[i])
        for i, (src, dst) in enumerate(zip(given, held))
    ]
    for i in (8, 9, 10, 0, 4, 1, 5, 2, 6, 3, 7):
        loads[i].start()
    for i in (8, 9, 10):
        loads[i].wait()
    h, da, dl = (held[i][...] for i in (8, 9, 10))
    stores = []
    for i in range(4):
        part = quarter_of(me, i, size)
        rows = (part, slice(None))
        cols = (slice(None), part)
        loads[i].wait()
        x = held[i][...]
        vg[part, :] = dot(x, da, TN).astype(BF16)
        stores.append(fetch(vg, gg, sem.at[0, i], rows))
        vu[part, :] = dot(x, dl, TN).astype(BF16)
        stores.append(fetch(vu, gu, sem.at[1, i], rows))
        loads[4 + i].wait()
        vd[:, part] = dot(h, held[4 + i][...], TN).astype(BF16)
        stores.append(fetch(vd, gd, sem.at[2, i], cols))
    for store in stores:
        store.wait()


def grads(xs, ds, hidden, dact, dlin):
    rows, size = xs[0].shape
    ff = hidden.shape[1]
    d = 4 * size
    return pl.pallas_call(
        grads_kernel,
        out_shape=(
            jax.ShapeDtypeStruct((d, ff), BF16),
            jax.ShapeDtypeStruct((d, ff), BF16),
            jax.ShapeDtypeStruct((ff, d), BF16),
        ),
        in_specs=[hspec()] * 11,
        out_specs=(hspec(),) * 3,
        scratch_shapes=[pltpu.VMEM((rows, size), BF16)] * 8
        + [pltpu.VMEM((rows, ff), BF16)] * 3
        + [
            pltpu.VMEM((d, ff), BF16),
            pltpu.VMEM((d, ff), BF16),
            pltpu.VMEM((ff, d), BF16),
            pltpu.SemaphoreType.DMA((3, 4)),
            pltpu.SemaphoreType.DMA((11,)),
        ],
        compiler_params=params(32),
        cost_estimate=cost(6 * rows * d * ff, 6 * d * ff + 4 * rows * d),
        name="grads",
    )(*(fixed(v) for v in (*xs, *ds, hidden, dact, dlin)))


def total_kernel(after, keep, near, far, out):
    out[...] = (keep[...] + near[...].astype(F32) + far[...].astype(F32)).astype(BF16)


def total(after, keep, near, far):
    return pl.pallas_call(
        total_kernel,
        out_shape=jax.ShapeDtypeStruct(far.shape, BF16),
        in_specs=[aspec()] + [vspec()] * 3,
        out_specs=vspec(),
        compiler_params=params(),
        cost_estimate=cost(2 * far.size, 12 * far.size),
        name="total",
    )(after, keep, near, far)


def mix_kernel(back, w_hi, w_lo, sel, d_out, routes, mixed, dots):
    slots, tok = sel.shape
    topk = routes.shape[0]
    experts = slots // CAP
    o = back[...]
    mixed[...] = (dot(w_hi[...], o) + dot(w_lo[...], o)).astype(BF16)
    select = sel[...]
    per_slot = jnp.sum(dot(select, d_out[...]) * o.astype(F32), axis=1, keepdims=True)
    spread = select.astype(F32) * per_slot
    per_expert = jnp.sum(spread.reshape(experts, CAP, tok), axis=1)
    match = routes[...][None] == lax.broadcasted_iota(jnp.int32, (experts, topk, tok), 0)
    dots[...] = jnp.sum(jnp.where(match, per_expert[:, None, :], 0.0), axis=0)


def mix(back, w_hi, w_lo, sel, d_out, routes_t):
    slots, quarter = back.shape
    topk, tok = routes_t.shape
    return pl.pallas_call(
        mix_kernel,
        out_shape=(
            jax.ShapeDtypeStruct((tok, quarter), BF16),
            jax.ShapeDtypeStruct((topk, tok), F32),
        ),
        in_specs=[vspec()] * 6,
        out_specs=(vspec(),) * 2,
        compiler_params=params(),
        cost_estimate=cost(6 * slots * tok * quarter, 6 * tok * quarter),
        name="mix",
    )(back, w_hi, w_lo, sel, d_out, routes_t)


def collect_kernel(back, pick, d_tokens):
    d_tokens[...] = dot(pick[...], back[...]).astype(BF16)


def collect(back, pick):
    slots, quarter = back.shape
    tok = pick.shape[0]
    return pl.pallas_call(
        collect_kernel,
        out_shape=jax.ShapeDtypeStruct((tok, quarter), BF16),
        in_specs=[vspec()] * 2,
        out_specs=vspec(),
        compiler_params=params(),
        cost_estimate=cost(2 * slots * tok * quarter, 4 * tok * quarter),
        name="collect",
    )(back, pick)


def swap(x, flip):
    return lax.ppermute(x, "tp", [(i, i ^ flip) for i in range(4)])


def exchange(x):
    return lax.all_to_all(x, "ctx", split_axis=0, concat_axis=0, tiled=True)


def gather(own):
    near = swap(own, 1)
    far = swap(own, 2)
    return (own, near, far, swap(far, 1))


def plus(keep, *others):
    return sum((o.astype(F32) for o in others), keep).astype(BF16)


def on_device(tokens, routes, gates, w_gate, w_up, w_down, d_out):
    tok, quarter = tokens.shape
    sources = lax.axis_size("ctx")
    experts = sources * w_gate.shape[0]
    slots = experts * CAP
    rows = sources * CAP
    routes_t = routes.T
    outgoing, sel, pick, w_hi, w_lo = dispatch(routes_t, gates.T, tokens, d_out, experts)
    arrived = exchange(outgoing)
    xq = gather(arrived[:, :CAP].reshape(rows, quarter))
    dq = gather(arrived[:, CAP:].reshape(rows, quarter))
    act, lin, hidden, vg, vu, vd, send_far, send_near, keep_far, keep_own = forward(
        xq, w_gate[0], w_up[0], w_down[0]
    )
    half_out = plus(keep_far, swap(send_far, 1))
    near_out = swap(send_near, 1)
    dact, dlin = hidden_grad(dq, act, lin, vd)
    send_dx_far, keep_dx_far = input_grad((3, 2), half_out, dact, dlin, vg, vu)
    far_out = swap(half_out, 2)
    half_dx = plus(keep_dx_far, swap(send_dx_far, 1))
    send_dx_near, keep_dx_own = input_grad((1, 0), send_dx_far, dact, dlin, vg, vu)
    far_dx = swap(half_dx, 2)
    near_dx = swap(send_dx_near, 1)
    out_rows = plus(keep_own, near_out, far_out)
    back_out = exchange(out_rows.reshape(sources, CAP, quarter)).reshape(slots, quarter)
    grad_gate, grad_up, grad_down = grads(xq, dq, hidden, dact, dlin)
    dx_rows = total(fixed(grad_gate), keep_dx_own, near_dx, far_dx)
    back_dx = exchange(dx_rows.reshape(sources, CAP, quarter)).reshape(slots, quarter)
    mixed, dots = mix(back_out, w_hi, w_lo, sel, d_out, routes_t)
    dots = dots + swap(dots, 1)
    dots = dots + swap(dots, 2)
    d_tokens = collect(back_dx, pick)
    return (mixed, d_tokens, dots.T, grad_gate[None], grad_up[None], grad_down[None])


def solution(mesh):
    placed = (
        P("ctx", "tp"),
        P("ctx", None),
        P("ctx", None),
        P("ctx", None, "tp"),
        P("ctx", None, "tp"),
        P("ctx", "tp", None),
        P("ctx", "tp"),
    )
    return jax.shard_map(
        on_device,
        mesh=mesh,
        in_specs=placed,
        out_specs=(
            P("ctx", "tp"),
            P("ctx", "tp"),
            P("ctx", None),
            P("ctx", None, "tp"),
            P("ctx", None, "tp"),
            P("ctx", "tp", None),
        ),
        check_vma=False,
    )
```

```python
import functools

import jax
import jax.numpy as jnp
from jax import lax
from jax.experimental import pallas as pl
from jax.experimental.pallas import tpu as pltpu
from jax.sharding import PartitionSpec as P

CAP = 16
F32 = jnp.float32
BF16 = jnp.bfloat16
NN = (((1,), (0,)), ((), ()))
NT = (((1,), (1,)), ((), ()))
TN = (((0,), (0,)), ((), ()))


def dot(a, b, dims=NN):
    return lax.dot_general(a, b, dims, preferred_element_type=F32)


def params(mib=16):
    return pltpu.CompilerParams(vmem_limit_bytes=mib * 1024 * 1024)


def cost(flops, nbytes):
    return pl.CostEstimate(flops=flops, bytes_accessed=nbytes, transcendentals=0)


def vspec():
    return pl.BlockSpec(memory_space=pltpu.VMEM)


def hspec():
    return pl.BlockSpec(memory_space=pltpu.HBM)


def aspec():
    return pl.BlockSpec(memory_space=pl.ANY)


def fixed(x):
    return pltpu.with_memory_space_constraint(x, pltpu.HBM)


def step(place, count):
    return (count - place) & (count - 1)


def relative(experts, topk, tok):
    place = lax.broadcasted_iota(jnp.int32, (experts, topk, tok), 0)
    return step(place, experts) ^ lax.axis_index("ctx")


def dispatch_kernel(experts, *refs):
    routes_in, gates_in, tokens_in, d_in = refs[:4]
    outs = refs[4 : 4 + experts]
    sel, pick, w_hi, w_lo, routes, gates, tokens, d_out, sem = refs[4 + experts :]
    topk, tok = routes.shape
    slots = experts * CAP
    loads = [
        pltpu.make_async_copy(src, dst, sem.at[i])
        for i, (src, dst) in enumerate(
            ((routes_in, routes), (gates_in, gates), (tokens_in, tokens), (d_in, d_out))
        )
    ]
    for load in loads:
        load.start()
    loads[0].wait()
    loads[1].wait()
    match = routes[...][None] == relative(experts, topk, tok)
    hit = jnp.sum(jnp.where(match, 1.0, 0.0), axis=1)
    gate = jnp.sum(jnp.where(match, gates[...][None], 0.0), axis=1)
    earlier = lax.broadcasted_iota(jnp.int32, (tok, tok), 0) < lax.broadcasted_iota(
        jnp.int32, (tok, tok), 1
    )
    before = dot(hit.astype(BF16), jnp.where(earlier, 1.0, 0.0).astype(BF16))
    place = jnp.where(hit > 0.0, before, -1.0)[:, None, :]
    row = lax.broadcasted_iota(jnp.int32, (experts, CAP, tok), 1).astype(F32)
    chosen = jnp.where(place == row, 1.0, 0.0)
    weight = (chosen * gate[:, None, :]).reshape(slots, tok)
    chosen = chosen.reshape(slots, tok)
    select = chosen.astype(BF16)
    loads[2].wait()
    x = dot(select, tokens[...]).astype(BF16)
    slot_gate = jnp.sum(weight, axis=1, keepdims=True)
    loads[3].wait()
    d = (slot_gate * dot(select, d_out[...])).astype(BF16)
    for e, out in enumerate(outs):
        out[:CAP] = x[e * CAP : (e + 1) * CAP]
        out[CAP:] = d[e * CAP : (e + 1) * CAP]
    sel[...] = select
    pick[...] = chosen.T.astype(BF16)
    back = weight.T
    high = back.astype(BF16)
    w_hi[...] = high
    w_lo[...] = (back - high.astype(F32)).astype(BF16)


def dispatch(routes_t, gates_t, tokens, d_out, experts):
    tok, quarter = tokens.shape
    slots = experts * CAP
    results = pl.pallas_call(
        functools.partial(dispatch_kernel, experts),
        out_shape=(jax.ShapeDtypeStruct((2 * CAP, quarter), BF16),) * experts
        + (
            jax.ShapeDtypeStruct((slots, tok), BF16),
            jax.ShapeDtypeStruct((tok, slots), BF16),
            jax.ShapeDtypeStruct((tok, slots), BF16),
            jax.ShapeDtypeStruct((tok, slots), BF16),
        ),
        in_specs=[hspec()] * 4,
        out_specs=(vspec(),) * (experts + 4),
        scratch_shapes=[
            pltpu.VMEM(routes_t.shape, jnp.int32),
            pltpu.VMEM(gates_t.shape, F32),
            pltpu.VMEM(tokens.shape, BF16),
            pltpu.VMEM(d_out.shape, BF16),
            pltpu.SemaphoreType.DMA((4,)),
        ],
        compiler_params=params(),
        cost_estimate=cost(4 * slots * tok * quarter, 8 * tok * quarter),
        name="dispatch",
    )(*(fixed(v) for v in (routes_t, gates_t, tokens, d_out)))
    return results[:experts], results[experts:]


def quarter_of(me, flip, size):
    return pl.ds(pl.multiple_of((me ^ flip) * size, size), size)


def fetch(src, dst, sem, part):
    copy = pltpu.make_async_copy(src.at[part], dst.at[part], sem)
    copy.start()
    return copy


def load_kernel(after, wg, wu, wd, vg, vu, vd, sem):
    rows = wg.shape[0] // 4
    copies = []
    for i in range(4):
        part = (pl.ds(i * rows, rows), slice(None))
        cols = (slice(None), pl.ds(i * rows, rows))
        copies.append(fetch(wg, vg, sem.at[0, i], part))
        copies.append(fetch(wu, vu, sem.at[1, i], part))
        copies.append(fetch(wd, vd, sem.at[2, i], cols))
    for copy in copies:
        copy.wait()


def load(after, *weights):
    return pl.pallas_call(
        load_kernel,
        out_shape=tuple(jax.ShapeDtypeStruct(w.shape, w.dtype) for w in weights),
        in_specs=[aspec()] + [hspec()] * 3,
        out_specs=(vspec(),) * 3,
        scratch_shapes=[pltpu.SemaphoreType.DMA((3, 4))],
        compiler_params=params(4),
        cost_estimate=cost(0, 0),
        name="load",
    )(after, *(fixed(w) for w in weights))


def pass_kernel(after, x, out):
    out[...] = x[...]


def pass_on(after, x):
    return pl.pallas_call(
        pass_kernel,
        out_shape=jax.ShapeDtypeStruct(x.shape, x.dtype),
        in_specs=[aspec(), vspec()],
        out_specs=vspec(),
        compiler_params=params(4),
        cost_estimate=cost(0, 0),
        name="pass_on",
    )(after, x)


def forward_kernel(
    x0, x1, x2, x3, vg, vu, vd, act, lin, hidden, send_far, send_near, keep_far, keep_own
):
    me = lax.axis_index("tp")
    size = x0.shape[1]
    xs = (x0, x1, x2, x3)
    a = b = None
    for i in range(4):
        part = quarter_of(me, i, size)
        x = xs[i][...]
        pa = dot(x, vg[part, :])
        pb = dot(x, vu[part, :])
        a = pa if a is None else a + pa
        b = pb if b is None else b + pb
    act[...] = a
    lin[...] = b
    h = (a * jax.nn.sigmoid(a) * b).astype(BF16)
    hidden[...] = h
    for i, out in ((3, send_far), (2, keep_far), (1, send_near), (0, keep_own)):
        out[...] = dot(h, vd[:, quarter_of(me, i, size)]).astype(out.dtype)


def forward(xs, vg, vu, vd):
    rows, size = xs[0].shape
    d, ff = vg.shape
    return pl.pallas_call(
        forward_kernel,
        out_shape=(
            jax.ShapeDtypeStruct((rows, ff), F32),
            jax.ShapeDtypeStruct((rows, ff), F32),
            jax.ShapeDtypeStruct((rows, ff), BF16),
            jax.ShapeDtypeStruct((rows, size), BF16),
            jax.ShapeDtypeStruct((rows, size), BF16),
            jax.ShapeDtypeStruct((rows, size), F32),
            jax.ShapeDtypeStruct((rows, size), F32),
        ),
        in_specs=[vspec()] * 7,
        out_specs=(vspec(),) * 7,
        compiler_params=params(),
        cost_estimate=cost(0, 0),
        name="forward",
    )(*xs, vg, vu, vd)


def hidden_grad_kernel(d0, d1, d2, d3, act, lin, hidden, vd, dact, dlin, dots):
    me = lax.axis_index("tp")
    rows, size = d0.shape
    ds = (d0, d1, d2, d3)
    dhid = None
    for i in range(4):
        p = dot(ds[i][...], vd[:, quarter_of(me, i, size)], NT)
        dhid = p if dhid is None else dhid + p
    a = act[...]
    s = jax.nn.sigmoid(a)
    dlin[...] = (dhid * (a * s)).astype(BF16)
    dact[...] = (dhid * lin[...] * s * (1.0 + a * (1.0 - s))).astype(BF16)
    per_row = jnp.sum(dhid * hidden[...].astype(F32), axis=1, keepdims=True)
    dots[...] = jnp.broadcast_to(per_row, (rows, 128)).T[:8]


def hidden_grad(ds, act, lin, hidden, vd):
    rows, size = ds[0].shape
    ff, d = vd.shape
    return pl.pallas_call(
        hidden_grad_kernel,
        out_shape=(
            jax.ShapeDtypeStruct((rows, ff), BF16),
            jax.ShapeDtypeStruct((rows, ff), BF16),
            jax.ShapeDtypeStruct((8, rows), F32),
        ),
        in_specs=[vspec()] * 8,
        out_specs=(vspec(),) * 3,
        compiler_params=params(),
        cost_estimate=cost(0, 0),
        name="hidden_grad",
    )(*ds, act, lin, hidden, vd)


def input_grad_kernel(flips, after, dact, dlin, vg, vu, send, keep):
    me = lax.axis_index("tp")
    size = send.shape[1]
    da = dact[...]
    dl = dlin[...]
    for i, out in zip(flips, (send, keep)):
        part = quarter_of(me, i, size)
        p = dot(da, vg[part, :], NT) + dot(dl, vu[part, :], NT)
        out[...] = p.astype(out.dtype)


def input_grad(flips, after, dact, dlin, vg, vu):
    rows, ff = dact.shape
    d = vg.shape[0]
    return pl.pallas_call(
        functools.partial(input_grad_kernel, flips),
        out_shape=(
            jax.ShapeDtypeStruct((rows, d // 4), BF16),
            jax.ShapeDtypeStruct((rows, d // 4), F32),
        ),
        in_specs=[aspec()] + [vspec()] * 4,
        out_specs=(vspec(),) * 2,
        compiler_params=params(),
        cost_estimate=cost(0, 0),
        name="input_grad",
    )(after, dact, dlin, vg, vu)


def grads_kernel(*refs):
    given, (gg, gu, gd), held, (vg, vu, vd, sem, load_sem) = (
        refs[:11],
        refs[11:14],
        refs[14:25],
        refs[25:],
    )
    me = lax.axis_index("tp")
    size = given[0].shape[1]
    loads = [
        pltpu.make_async_copy(src, dst, load_sem.at[i])
        for i, (src, dst) in enumerate(zip(given, held))
    ]
    for i in (8, 9, 10, 0, 4, 1, 5, 2, 6, 3, 7):
        loads[i].start()
    for i in (8, 9, 10):
        loads[i].wait()
    h, da, dl = (held[i][...] for i in (8, 9, 10))
    stores = []
    for i in range(4):
        part = quarter_of(me, i, size)
        rows = (part, slice(None))
        cols = (slice(None), part)
        loads[i].wait()
        x = held[i][...]
        vg[part, :] = dot(x, da, TN).astype(BF16)
        stores.append(fetch(vg, gg, sem.at[0, i], rows))
        vu[part, :] = dot(x, dl, TN).astype(BF16)
        stores.append(fetch(vu, gu, sem.at[1, i], rows))
        loads[4 + i].wait()
        vd[:, part] = dot(h, held[4 + i][...], TN).astype(BF16)
        stores.append(fetch(vd, gd, sem.at[2, i], cols))
    for store in stores:
        store.wait()


def grads(xs, ds, hidden, dact, dlin):
    rows, size = xs[0].shape
    ff = hidden.shape[1]
    d = 4 * size
    return pl.pallas_call(
        grads_kernel,
        out_shape=(
            jax.ShapeDtypeStruct((d, ff), BF16),
            jax.ShapeDtypeStruct((d, ff), BF16),
            jax.ShapeDtypeStruct((ff, d), BF16),
        ),
        in_specs=[hspec()] * 11,
        out_specs=(hspec(),) * 3,
        scratch_shapes=[pltpu.VMEM((rows, size), BF16)] * 8
        + [pltpu.VMEM((rows, ff), BF16)] * 3
        + [
            pltpu.VMEM((d, ff), BF16),
            pltpu.VMEM((d, ff), BF16),
            pltpu.VMEM((ff, d), BF16),
            pltpu.SemaphoreType.DMA((3, 4)),
            pltpu.SemaphoreType.DMA((11,)),
        ],
        compiler_params=params(32),
        cost_estimate=cost(6 * rows * d * ff, 6 * d * ff),
        name="grads",
    )(*(fixed(v) for v in (*xs, *ds, hidden, dact, dlin)))


def total_kernel(after, o_keep, o_near, o_far, x_keep, x_near, x_far, dots, *outs):
    tiles, cap, lanes = outs[0].shape
    rows, size = o_keep.shape
    half = tiles // 2

    def place(at, value):
        value = value.astype(BF16)
        for e, out in enumerate(outs):
            out[at] = value[e * cap : (e + 1) * cap]

    for j in range(half):
        part = slice(j * lanes, (j + 1) * lanes)
        for base, (keep, near, far) in ((0, (o_keep, o_near, o_far)), (half, (x_keep, x_near, x_far))):
            place(base + j, keep[:, part] + near[:, part].astype(F32) + far[:, part].astype(F32))
    d = jnp.broadcast_to(dots[:1], (lanes, rows)).T
    high = d.astype(BF16).astype(F32)
    first = lax.broadcasted_iota(jnp.int32, (rows, lanes), 1) < lanes // 2
    place(tiles - 1, jnp.where(first, high, d - high))


def total(after, out_parts, dx_parts, dots):
    rows, size = out_parts[0].shape
    tiles = 2 * (size // 128) + 1
    count = rows // CAP
    return pl.pallas_call(
        total_kernel,
        out_shape=(jax.ShapeDtypeStruct((tiles, CAP, 128), BF16),) * count,
        in_specs=[aspec()] + [vspec()] * 7,
        out_specs=(vspec(),) * count,
        compiler_params=params(),
        cost_estimate=cost(0, 0),
        name="total",
    )(fixed(after), *out_parts, *dx_parts, dots)


def combine_kernel(*refs):
    w_hi, w_lo, pick, sel, routes, gates = refs[:6]
    back = refs[6:-3]
    mixed, d_tokens, d_gates = refs[-3:]
    tiles, cap, lanes = back[0].shape
    slots, tok = sel.shape
    topk = routes.shape[0]
    experts = len(back)
    half = tiles // 2

    def rows_of(first):
        return jnp.concatenate(
            [jnp.concatenate([b[first + j] for j in range(half)], axis=1) for b in back], axis=0
        )

    o = rows_of(0)
    mixed[...] = (dot(w_hi[...], o) + dot(w_lo[...], o)).astype(BF16)
    d_tokens[...] = dot(pick[...], rows_of(half)).astype(BF16)
    both = jnp.concatenate([b[tiles - 1] for b in back], axis=0).astype(F32)
    per_slot = both[:, :1] + both[:, lanes // 2 : lanes // 2 + 1]
    spread = sel[...].astype(F32) * per_slot
    per_expert = jnp.sum(spread.reshape(experts, cap, tok), axis=1)
    match = routes[...][None] == relative(experts, topk, tok)
    scaled = jnp.sum(jnp.where(match, per_expert[:, None, :], 0.0), axis=0)
    d_gates[...] = scaled / gates[...]


def combine(back, w_hi, w_lo, pick, sel, routes_t, gates_t):
    quarter = back[0].shape[0] // 2 * 128
    topk, tok = routes_t.shape
    return pl.pallas_call(
        combine_kernel,
        out_shape=(
            jax.ShapeDtypeStruct((tok, quarter), BF16),
            jax.ShapeDtypeStruct((tok, quarter), BF16),
            jax.ShapeDtypeStruct((topk, tok), F32),
        ),
        in_specs=[vspec()] * (6 + len(back)),
        out_specs=(vspec(),) * 3,
        compiler_params=params(),
        cost_estimate=cost(0, 0),
        name="combine",
    )(w_hi, w_lo, pick, sel, routes_t, gates_t, *back)


def swap(x, flip):
    return lax.ppermute(x, "tp", [(i, i ^ flip) for i in range(4)])


def exchange(parts):
    count = len(parts)
    assert count & (count - 1) == 0
    return [parts[0]] + [
        lax.ppermute(parts[p], "ctx", [(i, i ^ step(p, count)) for i in range(count)])
        for p in range(1, count)
    ]


def gather(own):
    near = swap(own, 1)
    far = swap(own, 2)
    return (own, near, far, swap(far, 1))


def plus(keep, *others):
    return sum((o.astype(F32) for o in others), keep).astype(BF16)


def on_device(tokens, routes, gates, w_gate, w_up, w_down, d_out):
    tok, quarter = tokens.shape
    sources = lax.axis_size("ctx")
    experts = sources * w_gate.shape[0]
    slots = experts * CAP
    rows = sources * CAP
    routes_t = routes.T
    gates_t = gates.T
    outgoing, (sel, pick, w_hi, w_lo) = dispatch(routes_t, gates_t, tokens, d_out, experts)
    arrived = exchange(outgoing)
    x0 = jnp.concatenate([part[:CAP] for part in arrived], axis=0)
    x2 = swap(x0, 2)
    dq = gather(jnp.concatenate([part[CAP:] for part in arrived], axis=0))
    vg, vu, vd = load(x0, w_gate[0], w_up[0], w_down[0])
    xq = (x0, swap(x0, 1), x2, swap(pass_on(vg, x2), 1))
    act, lin, hidden, send_far, send_near, keep_far, keep_own = forward(xq, vg, vu, vd)
    half_out = plus(keep_far, swap(send_far, 1))
    near_out = swap(send_near, 1)
    dact, dlin, dots = hidden_grad(dq, act, lin, hidden, vd)
    send_dx_far, keep_dx_far = input_grad((3, 2), half_out, dact, dlin, vg, vu)
    far_out = swap(half_out, 2)
    half_dx = plus(keep_dx_far, swap(send_dx_far, 1))
    send_dx_near, keep_dx_own = input_grad((1, 0), send_dx_far, dact, dlin, vg, vu)
    far_dx = swap(half_dx, 2)
    near_dx = swap(send_dx_near, 1)
    dots = dots + swap(dots, 1)
    dots = dots + swap(dots, 2)
    grad_gate, grad_up, grad_down = grads(xq, dq, hidden, dact, dlin)
    back = exchange(
        total(grad_gate, (keep_own, near_out, far_out), (keep_dx_own, near_dx, far_dx), dots)
    )
    mixed, d_tokens, d_gates = combine(back, w_hi, w_lo, pick, sel, routes_t, gates_t)
    return (mixed, d_tokens, d_gates.T, grad_gate[None], grad_up[None], grad_down[None])


def solution(mesh):
    placed = (
        P("ctx", "tp"),
        P("ctx", None),
        P("ctx", None),
        P("ctx", None, "tp"),
        P("ctx", None, "tp"),
        P("ctx", "tp", None),
        P("ctx", "tp"),
    )
    return jax.shard_map(
        on_device,
        mesh=mesh,
        in_specs=placed,
        out_specs=(
            P("ctx", "tp"),
            P("ctx", "tp"),
            P("ctx", None),
            P("ctx", None, "tp"),
            P("ctx", None, "tp"),
            P("ctx", "tp", None),
        ),
        check_vma=False,
    )
```

```python
import functools

import jax
import jax.numpy as jnp
from jax import lax
from jax.experimental import pallas as pl
from jax.experimental.pallas import tpu as pltpu
from jax.sharding import PartitionSpec as P

CAP = 16
LANES = 128
F32 = jnp.float32
BF16 = jnp.bfloat16
NN = (((1,), (0,)), ((), ()))
NT = (((1,), (1,)), ((), ()))
TN = (((0,), (0,)), ((), ()))


def dot(a, b, dims=NN):
    return lax.dot_general(a, b, dims, preferred_element_type=F32)


def vspec():
    return pl.BlockSpec(memory_space=pltpu.VMEM)


def hspec():
    return pl.BlockSpec(memory_space=pltpu.HBM)


def aspec():
    return pl.BlockSpec(memory_space=pl.ANY)


def fixed(x):
    return pltpu.with_memory_space_constraint(x, pltpu.HBM)


def array(shape, dtype=BF16):
    return jax.ShapeDtypeStruct(shape, dtype)


def call(kernel, name, out_shape, in_specs, out_spec, scratch=(), mib=16, flops=0, nbytes=0):
    out_specs = (out_spec,) * len(out_shape) if isinstance(out_shape, tuple) else out_spec
    return pl.pallas_call(
        kernel,
        out_shape=out_shape,
        in_specs=in_specs,
        out_specs=out_specs,
        scratch_shapes=list(scratch),
        compiler_params=pltpu.CompilerParams(vmem_limit_bytes=mib * 1024 * 1024),
        cost_estimate=pl.CostEstimate(flops=flops, bytes_accessed=nbytes, transcendentals=0),
        name=name,
    )


def fetch(src, dst, sem):
    copy = pltpu.make_async_copy(src, dst, sem)
    copy.start()
    return copy


def steps(count):
    return [0] + sorted(range(1, count), key=lambda s: ([3,6,7,1,2,4,5].index(s) if count == 8 else -s))


def groups(count):
    if count == 8:
        listed = [[7, 6], [3, 5, 4], [2, 1, 0]]
    else:
        far = sorted(range(1, count), reverse=True) + [0]
        third = -(-count // 3)
        listed = [far[:third], far[third : 2 * third], far[2 * third :]]
    order = steps(count)
    return [[order.index(s) for s in group] for group in listed]


def relative(experts, topk, tok):
    place = lax.broadcasted_iota(jnp.int32, (experts, topk, tok), 0)
    distance = jnp.zeros_like(place)
    for p, s in enumerate(steps(experts)):
        distance = jnp.where(place == p, s, distance)
    return distance ^ lax.axis_index("ctx")


def dispatch_kernel(experts, *refs):
    routes_in, gates_in, tokens_in, d_in = refs[:4]
    outs = refs[4 : 4 + experts]
    sel, pick, w_hi, w_lo, routes, gates, tokens, d_out, sem = refs[4 + experts :]
    topk, tok = routes.shape
    slots = experts * CAP
    pairs = ((routes_in, routes), (gates_in, gates), (tokens_in, tokens), (d_in, d_out))
    loads = [fetch(src, dst, sem.at[i]) for i, (src, dst) in enumerate(pairs)]
    loads[0].wait()
    loads[1].wait()
    match = routes[...][None] == relative(experts, topk, tok)
    hit = jnp.sum(jnp.where(match, 1.0, 0.0), axis=1)
    gate = jnp.sum(jnp.where(match, gates[...][None], 0.0), axis=1)
    earlier = lax.broadcasted_iota(jnp.int32, (tok, tok), 0) < lax.broadcasted_iota(
        jnp.int32, (tok, tok), 1
    )
    before = dot(hit.astype(BF16), jnp.where(earlier, 1.0, 0.0).astype(BF16))
    place = jnp.where(hit > 0.0, before, -1.0)[:, None, :]
    row = lax.broadcasted_iota(jnp.int32, (experts, CAP, tok), 1).astype(F32)
    chosen = jnp.where(place == row, 1.0, 0.0)
    weight = (chosen * gate[:, None, :]).reshape(slots, tok)
    chosen = chosen.reshape(slots, tok)
    select = chosen.astype(BF16)
    loads[2].wait()
    x = dot(select, tokens[...]).astype(BF16)
    slot_gate = jnp.sum(weight, axis=1, keepdims=True)
    loads[3].wait()
    d = (slot_gate * dot(select, d_out[...])).astype(BF16)
    for e, out in enumerate(outs):
        out[0] = x[e * CAP : (e + 1) * CAP]
        out[1] = d[e * CAP : (e + 1) * CAP]
    sel[...] = select
    pick[...] = chosen.T.astype(BF16)
    back = weight.T
    high = back.astype(BF16)
    w_hi[...] = high
    w_lo[...] = (back - high.astype(F32)).astype(BF16)


def dispatch(routes_t, gates_t, tokens, d_out, experts):
    tok, quarter = tokens.shape
    slots = experts * CAP
    results = call(
        functools.partial(dispatch_kernel, experts),
        "dispatch",
        (array((2, CAP, quarter)),) * experts
        + (array((slots, tok)),)
        + (array((tok, slots)),) * 3,
        [hspec()] * 4,
        vspec(),
        [
            pltpu.VMEM(routes_t.shape, jnp.int32),
            pltpu.VMEM(gates_t.shape, F32),
            pltpu.VMEM(tokens.shape, BF16),
            pltpu.VMEM(d_out.shape, BF16),
            pltpu.SemaphoreType.DMA((4,)),
        ],
    )(*(fixed(v) for v in (routes_t, gates_t, tokens, d_out)))
    return results[:experts], results[experts:]


def quarter_of(me, flip, size):
    return pl.ds(pl.multiple_of((me ^ flip) * size, size), size)


def load_kernel(after, wg, wu, wd, vg, vu, vd, sem):
    rows = wg.shape[0] // 4
    copies = []
    for i in range(4):
        part = (pl.ds(i * rows, rows), slice(None))
        cols = (slice(None), pl.ds(i * rows, rows))
        copies.append(fetch(wg.at[part], vg.at[part], sem.at[0, i]))
        copies.append(fetch(wu.at[part], vu.at[part], sem.at[1, i]))
        copies.append(fetch(wd.at[cols], vd.at[cols], sem.at[2, i]))
    for copy in copies:
        copy.wait()


def load(after, *weights):
    return call(
        load_kernel,
        "load",
        tuple(array(w.shape) for w in weights),
        [aspec()] + [hspec()] * 3,
        vspec(),
        [pltpu.SemaphoreType.DMA((3, 4))],
        mib=4,
    )(after, *(fixed(w) for w in weights))


def pass_kernel(after, x, *outs):
    count = outs[0].shape[0]
    for n, out in enumerate(outs):
        out[...] = x[n * count : (n + 1) * count]


def pass_on(after, x, pieces):
    shape = (x.shape[0] // pieces, *x.shape[1:])
    out_shape = (array(shape),) * pieces
    return call(pass_kernel, "pass_on", out_shape, [aspec(), vspec()], vspec(), mib=4)(after, x)


def rows_of(first, rest, which):
    size = first.shape[3]
    return jnp.concatenate(
        [first[:, which].reshape(-1, size), rest[...].reshape(-1, size)], axis=0
    )


def forward_kernel(after, after_too, *refs):
    firsts, rests = refs[:4], refs[4:8]
    vg, vu, vd, act, lin, hidden, send, keep_far, keep_own = refs[8:]
    me = lax.axis_index("tp")
    size = firsts[0].shape[3]
    a = b = None
    for i in range(4):
        part = quarter_of(me, i, size)
        x = rows_of(firsts[i], rests[i], 0)
        pa = dot(x, vg[part, :])
        pb = dot(x, vu[part, :])
        a = pa if a is None else a + pa
        b = pb if b is None else b + pb
    act[...] = a
    lin[...] = b
    h = (a * jax.nn.sigmoid(a) * b).astype(BF16)
    hidden[...] = h
    for i, out in ((3, send.at[0]), (1, send.at[1]), (2, keep_far), (0, keep_own)):
        out[...] = dot(h, vd[:, quarter_of(me, i, size)]).astype(out.dtype)


def forward(after, after_too, firsts, rests, vg, vu, vd):
    size = firsts[0].shape[3]
    rows = (firsts[0].shape[0] + rests[0].shape[0]) * CAP
    ff = vg.shape[1]
    return call(
        forward_kernel,
        "forward",
        (array((rows, ff), F32),) * 2
        + (array((rows, ff)),)
        + (array((2, rows, size)),)
        + (array((rows, size), F32),) * 2,
        [aspec()] * 2 + [vspec()] * 11,
        vspec(),
    )(after, after_too, *firsts, *rests, vg, vu, vd)


def hidden_grad_kernel(*refs):
    firsts, rests = refs[:4], refs[4:8]
    act, lin, hidden, vd, dact, dlin, dots = refs[8:]
    me = lax.axis_index("tp")
    size = firsts[0].shape[3]
    rows = act.shape[0]
    dhid = None
    for i in range(4):
        p = dot(rows_of(firsts[i], rests[i], 1), vd[:, quarter_of(me, i, size)], NT)
        dhid = p if dhid is None else dhid + p
    a = act[...]
    s = jax.nn.sigmoid(a)
    dlin[...] = (dhid * (a * s)).astype(BF16)
    dact[...] = (dhid * lin[...] * s * (1.0 + a * (1.0 - s))).astype(BF16)
    per_row = jnp.sum(dhid * hidden[...].astype(F32), axis=1, keepdims=True)
    dots[...] = jnp.broadcast_to(per_row, (rows, LANES)).T[:8]


def hidden_grad(firsts, rests, act, lin, hidden, vd):
    rows, ff = act.shape
    return call(
        hidden_grad_kernel,
        "hidden_grad",
        (array((rows, ff)),) * 2 + (array((8, rows), F32),),
        [vspec()] * 12,
        vspec(),
    )(*firsts, *rests, act, lin, hidden, vd)


def pack_dots(dots, size):
    wide = jnp.concatenate([dots, jnp.zeros((8, size - dots.shape[1]), F32)], axis=1)
    high = wide.astype(BF16).astype(F32)
    top = lax.broadcasted_iota(jnp.int32, wide.shape, 0) == 0
    block = jnp.where(top, high, wide - high)
    return jnp.concatenate([block, block], axis=0).astype(BF16)


def unpack_dots(block, rows):
    block = block.astype(F32)
    return jnp.broadcast_to(block[0:1, :rows] + block[1:2, :rows], (8, rows))


def input_grad_kernel(flips, after, dots, dact, dlin, vg, vu, send, keep):
    me = lax.axis_index("tp")
    rows, size = keep.shape
    da = dact[...]
    dl = dlin[...]
    for i, out in zip(flips, (send, keep)):
        part = quarter_of(me, i, size)
        p = dot(da, vg[part, :], NT) + dot(dl, vu[part, :], NT)
        out[:rows] = p.astype(out.dtype)
    if send.shape[0] > rows:
        send[rows:] = pack_dots(dots[...], size)


def input_grad(flips, after, dots, dact, dlin, vg, vu, more=0):
    rows = dact.shape[0]
    size = vg.shape[0] // 4
    return call(
        functools.partial(input_grad_kernel, flips),
        "input_grad",
        (array((rows + more, size)), array((rows, size), F32)),
        [aspec()] + [vspec()] * 5,
        vspec(),
    )(after, dots, dact, dlin, vg, vu)


def half_kernel(places, after, o_keep, o_near, x_keep, x_near, dots, out):
    rows, size = o_keep.shape
    count = len(places) * CAP
    for n, p in enumerate(places):
        span = slice(p * CAP, (p + 1) * CAP)
        o = o_keep[span] + o_near[0, span].astype(F32)
        x = x_keep[span] + x_near[span].astype(F32)
        out[n * CAP : (n + 1) * CAP] = o.astype(BF16)
        out[count + n * CAP : count + (n + 1) * CAP] = x.astype(BF16)
    if out.shape[0] > 2 * count:
        out[2 * count :] = pack_dots(dots[...] + unpack_dots(x_near[rows:], rows), size)


def half(after, places, o_keep, o_near, x_keep, x_near, dots, more=0):
    size = o_keep.shape[1]
    return call(
        functools.partial(half_kernel, places),
        "half",
        array((2 * CAP * len(places) + more, size)),
        [aspec()] + [vspec()] * 5,
        vspec(),
    )(after, o_keep, o_near, x_keep, x_near, dots)


def grads_kernel(which, count, after, *refs):
    firsts, rests = refs[:4], refs[4:8]
    given = refs[8 : 8 + count]
    outs = refs[8 + count : 8 + 2 * count]
    made = refs[8 + 2 * count : 8 + 3 * count]
    sem = refs[8 + 3 * count]
    me = lax.axis_index("tp")
    size = firsts[0].shape[3]
    values = [g[...] for g in given]
    stores = []
    for i in range(4):
        part = quarter_of(me, i, size)
        rows = rows_of(firsts[i], rests[i], which)
        for n in range(count):
            if which == 0:
                at = (part, slice(None))
                made[n][at] = dot(rows, values[n], TN).astype(BF16)
            else:
                at = (slice(None), part)
                made[n][at] = dot(values[n], rows, TN).astype(BF16)
            stores.append(fetch(made[n].at[at], outs[n].at[at], sem.at[n, i]))
    for copy in stores:
        copy.wait()


def grads(after, which, firsts, rests, given):
    size = firsts[0].shape[3]
    rows, ff = given[0].shape
    count = len(given)
    shape = (4 * size, ff) if which == 0 else (ff, 4 * size)
    return call(
        functools.partial(grads_kernel, which, count),
        "grads",
        (array(shape),) * count,
        [aspec()] + [vspec()] * (8 + count),
        hspec(),
        [pltpu.VMEM(shape, BF16)] * count + [pltpu.SemaphoreType.DMA((count, 4))],
        mib=20,
        flops=2 * count * rows * ff * 4 * size,
        nbytes=2 * count * ff * 4 * size,
    )(after, *firsts, *rests, *given)


def total_kernel(places, after, o_keep, o_near, x_keep, x_near, far, dots, x_send, first, *outs):
    tiles, cap, lanes = outs[0].shape
    count = len(outs) * cap
    rows, size = o_keep.shape
    middle = tiles // 2
    d = dots[...] + unpack_dots(x_send[rows:], rows) + unpack_dots(first[first.shape[0] - 16 :], rows)
    d = jnp.broadcast_to(d[:1], (lanes, rows)).T
    high = d.astype(BF16).astype(F32)
    left = lax.broadcasted_iota(jnp.int32, (rows, lanes), 1) < lanes // 2
    d = jnp.where(left, high, d - high)
    for n, (p, out) in enumerate(zip(places, outs)):
        span = slice(p * cap, (p + 1) * cap)
        at = slice(n * cap, (n + 1) * cap)
        also = slice(count + n * cap, count + (n + 1) * cap)
        for j in range(middle):
            part = slice(j * lanes, (j + 1) * lanes)
            o = o_near[1, span, part].astype(F32) + far[at, part].astype(F32)
            out[j] = (o_keep[span, part] + o).astype(BF16)
            x = x_near[span, part].astype(F32) + far[also, part].astype(F32)
            out[middle + j] = (x_keep[span, part] + x).astype(BF16)
        out[tiles - 1] = d[span].astype(BF16)


def total(after, places, keeps, far, sums):
    size = far.shape[1]
    tiles = 2 * (size // LANES) + 1
    return call(
        functools.partial(total_kernel, places),
        "total",
        (array((tiles, CAP, LANES)),) * len(places),
        [aspec()] + [vspec()] * 8,
        vspec(),
    )(after, *keeps, far, *sums)


def combine_kernel(places, *refs):
    w_hi, w_lo, pick, sel, routes, gates = refs[:6]
    back = [refs[6 + places.index(p)] for p in range(len(places))]
    mixed, d_tokens, d_gates = refs[-3:]
    tiles, cap, lanes = back[0].shape
    slots, tok = sel.shape
    topk = routes.shape[0]
    experts = len(back)
    middle = tiles // 2

    def all_rows(first):
        return jnp.concatenate(
            [jnp.concatenate([b[first + j] for j in range(middle)], axis=1) for b in back], axis=0
        )

    o = all_rows(0)
    mixed[...] = (dot(w_hi[...], o) + dot(w_lo[...], o)).astype(BF16)
    d_tokens[...] = dot(pick[...], all_rows(middle)).astype(BF16)
    both = jnp.concatenate([b[tiles - 1] for b in back], axis=0).astype(F32)
    per_slot = both[:, :1] + both[:, lanes // 2 : lanes // 2 + 1]
    spread = sel[...].astype(F32) * per_slot
    per_expert = jnp.sum(spread.reshape(experts, cap, tok), axis=1)
    match = routes[...][None] == relative(experts, topk, tok)
    scaled = jnp.sum(jnp.where(match, per_expert[:, None, :], 0.0), axis=0)
    d_gates[...] = scaled / gates[...]


def combine(places, back, w_hi, w_lo, pick, sel, routes_t, gates_t):
    quarter = back[0].shape[0] // 2 * LANES
    topk, tok = routes_t.shape
    return call(
        functools.partial(combine_kernel, places),
        "combine",
        (array((tok, quarter)), array((tok, quarter)), array((topk, tok), F32)),
        [vspec()] * (6 + len(back)),
        vspec(),
    )(w_hi, w_lo, pick, sel, routes_t, gates_t, *back)


def swap(x, flip):
    return lax.ppermute(x, "tp", [(i, i ^ flip) for i in range(4)])


def exchange(parts, places, count):
    assert count & (count - 1) == 0
    order = steps(count)
    return [
        lax.ppermute(part, "ctx", [(i, i ^ order[p]) for i in range(count)]) if p else part
        for part, p in zip(parts, places)
    ]


def on_device(tokens, routes, gates, w_gate, w_up, w_down, d_out):
    sources = lax.axis_size("ctx")
    routes_t, gates_t = routes.T, gates.T
    parts, (sel, pick, w_hi, w_lo) = dispatch(routes_t, gates_t, tokens, d_out, sources)
    got = exchange(parts, range(sources), sources)
    early = sources // 2
    cut = early * CAP
    rows = sources * CAP
    first = jnp.stack(got[:early])
    rest_x = jnp.stack([g[0] for g in got[early:]])
    rest_d = jnp.stack([g[1] for g in got[early:]])
    far_first = swap(first, 2)
    far_x = swap(rest_x, 2)
    far_d = swap(rest_d, 2)
    vg, vu, vd = load(first, w_gate[0], w_up[0], w_down[0])
    firsts = (first, swap(first, 1), far_first, swap(far_first, 1))
    across = jnp.concatenate([swap(piece, 1) for piece in pass_on(vg, far_x, 1)])
    xs = (rest_x, swap(rest_x, 1), far_x, across)
    ds = (rest_d, swap(rest_d, 1), far_d, swap(far_d, 1))

    act, lin, hidden, send, keep_far, keep_own = forward(ds[3], ds[1], firsts, xs, vg, vu, vd)
    near_out = swap(send, 1)
    dact, dlin, dots = hidden_grad(firsts, ds, act, lin, hidden, vd)
    send_dx, keep_dx = input_grad((3, 2), dots, dots, dact, dlin, vg, vu, more=16)
    near_send = swap(send_dx, 1)
    send_dx_near, keep_dx_own = input_grad((1, 0), send_dx, dots, dact, dlin, vg, vu)
    near_dx = swap(send_dx_near, 1)
    one, two, three = groups(sources)
    halves = (keep_far, near_out, keep_dx, near_send, dots)
    half_one = half(keep_dx_own, one, *halves, more=16)
    half_two = half(half_one, two, *halves)
    grad_gate, grad_up = grads(half_one, 0, firsts, xs, (dact, dlin))
    half_three = half(fixed(grad_gate), three, *halves)
    far_one, far_two, far_three = swap(half_one, 2), swap(half_two, 2), swap(half_three, 2)
    (grad_down,) = grads(half_one, 1, firsts, ds, (hidden,))
    keeps = (keep_own, near_out, keep_dx_own, near_dx)
    sums = (dots, near_send, far_one)
    back_one = total(fixed(grad_up), one, keeps, far_one, sums)
    back_two = total(back_one[0], two, keeps, far_two, sums)
    back_three = total(back_two[0], three, keeps, far_three, sums)
    places = [*one, *two, *three]
    back = exchange([*back_one, *back_two, *back_three], places, sources)
    mixed, d_tokens, d_gates = combine(places, back, w_hi, w_lo, pick, sel, routes_t, gates_t)
    return (mixed, d_tokens, d_gates.T, grad_gate[None], grad_up[None], grad_down[None])


def solution(mesh):
    placed = (
        P("ctx", "tp"),
        P("ctx", None),
        P("ctx", None),
        P("ctx", None, "tp"),
        P("ctx", None, "tp"),
        P("ctx", "tp", None),
        P("ctx", "tp"),
    )
    return jax.shard_map(
        on_device,
        mesh=mesh,
        in_specs=placed,
        out_specs=(
            P("ctx", "tp"),
            P("ctx", "tp"),
            P("ctx", None),
            P("ctx", None, "tp"),
            P("ctx", None, "tp"),
            P("ctx", "tp", None),
        ),
        check_vma=False,
    )
```

```python
import functools

import jax
import jax.numpy as jnp
from jax import lax
from jax.experimental import pallas as pl
from jax.experimental.pallas import tpu as pltpu
from jax.sharding import PartitionSpec as P

CAP = 16
LANES = 128
F32 = jnp.float32
BF16 = jnp.bfloat16
NN = (((1,), (0,)), ((), ()))
NT = (((1,), (1,)), ((), ()))
TN = (((0,), (0,)), ((), ()))


def dot(a, b, dims=NN):
    return lax.dot_general(a, b, dims, preferred_element_type=F32)


def vspec():
    return pl.BlockSpec(memory_space=pltpu.VMEM)


def hspec():
    return pl.BlockSpec(memory_space=pltpu.HBM)


def aspec():
    return pl.BlockSpec(memory_space=pl.ANY)


def fixed(x):
    return pltpu.with_memory_space_constraint(x, pltpu.HBM)


def array(shape, dtype=BF16):
    return jax.ShapeDtypeStruct(shape, dtype)


def call(kernel, name, out_shape, in_specs, out_spec, scratch=(), mib=16, flops=0, nbytes=0):
    out_specs = (out_spec,) * len(out_shape) if isinstance(out_shape, tuple) else out_spec
    return pl.pallas_call(
        kernel,
        out_shape=out_shape,
        in_specs=in_specs,
        out_specs=out_specs,
        scratch_shapes=list(scratch),
        compiler_params=pltpu.CompilerParams(vmem_limit_bytes=mib * 1024 * 1024),
        cost_estimate=pl.CostEstimate(flops=flops, bytes_accessed=nbytes, transcendentals=0),
        name=name,
    )


def fetch(src, dst, sem):
    copy = pltpu.make_async_copy(src, dst, sem)
    copy.start()
    return copy


def steps(count):
    return [0] + sorted(range(1, count), key=lambda s: ([2, 6, 7, 1, 3, 4, 5].index(s) if count == 8 else -s))


def groups(count):
    if count == 8:
        listed = [[7, 6], [3, 5, 4], [2, 1, 0]]
    else:
        far = sorted(range(1, count), reverse=True) + [0]
        third = -(-count // 3)
        listed = [far[:third], far[third : 2 * third], far[2 * third :]]
    order = steps(count)
    return [[order.index(s) for s in group] for group in listed]


def relative(experts, topk, tok):
    place = lax.broadcasted_iota(jnp.int32, (experts, topk, tok), 0)
    distance = jnp.zeros_like(place)
    for p, s in enumerate(steps(experts)):
        distance = jnp.where(place == p, s, distance)
    return distance ^ lax.axis_index("ctx")


def dispatch_kernel(experts, *refs):
    routes_in, gates_in, tokens_in, d_in = refs[:4]
    outs = refs[4 : 4 + experts]
    sel, weights, routes, gates, tokens, d_out, sem = refs[4 + experts :]
    topk, tok = routes.shape
    slots = experts * CAP
    pairs = ((routes_in, routes), (gates_in, gates), (tokens_in, tokens), (d_in, d_out))
    loads = [fetch(src, dst, sem.at[i]) for i, (src, dst) in enumerate(pairs)]
    loads[0].wait()
    loads[1].wait()
    match = routes[...][None] == relative(experts, topk, tok)
    hit = jnp.sum(jnp.where(match, 1.0, 0.0), axis=1)
    gate = jnp.sum(jnp.where(match, gates[...][None], 0.0), axis=1)
    earlier = lax.broadcasted_iota(jnp.int32, (tok, tok), 0) < lax.broadcasted_iota(
        jnp.int32, (tok, tok), 1
    )
    before = dot(hit.astype(BF16), jnp.where(earlier, 1.0, 0.0).astype(BF16))
    place = jnp.where(hit > 0.0, before, -1.0)[:, None, :]
    row = lax.broadcasted_iota(jnp.int32, (experts, CAP, tok), 1).astype(F32)
    chosen = jnp.where(place == row, 1.0, 0.0)
    weight = (chosen * gate[:, None, :]).reshape(slots, tok)
    chosen = chosen.reshape(slots, tok)
    select = chosen.astype(BF16)
    loads[2].wait()
    x = dot(select, tokens[...]).astype(BF16)
    slot_gate = jnp.sum(weight, axis=1, keepdims=True)
    loads[3].wait()
    d = (slot_gate * dot(select, d_out[...])).astype(BF16)
    for e, out in enumerate(outs):
        out[0] = x[e * CAP : (e + 1) * CAP]
        out[1] = d[e * CAP : (e + 1) * CAP]
    sel[...] = select
    weights[...] = weight


def dispatch(routes_t, gates_t, tokens, d_out, experts):
    tok, quarter = tokens.shape
    slots = experts * CAP
    results = call(
        functools.partial(dispatch_kernel, experts),
        "dispatch",
        (array((2, CAP, quarter)),) * experts
        + (array((slots, tok)), array((slots, tok), F32)),
        [hspec()] * 4,
        vspec(),
        [
            pltpu.VMEM(routes_t.shape, jnp.int32),
            pltpu.VMEM(gates_t.shape, F32),
            pltpu.VMEM(tokens.shape, BF16),
            pltpu.VMEM(d_out.shape, BF16),
            pltpu.SemaphoreType.DMA((4,)),
        ],
    )(*(fixed(v) for v in (routes_t, gates_t, tokens, d_out)))
    return results[:experts], results[experts:]


def turn_kernel(after, sel, weights, pick, mix):
    slots = sel.shape[0]
    pick[...] = sel[...].astype(F32).T.astype(BF16)
    back = weights[...].T
    high = back.astype(BF16)
    mix[:, :slots] = high
    mix[:, slots:] = (back - high.astype(F32)).astype(BF16)


def turn(after, sel, weights):
    slots, tok = sel.shape
    return call(
        turn_kernel,
        "turn",
        (array((tok, slots)), array((tok, 2 * slots))),
        [aspec()] + [vspec()] * 2,
        vspec(),
    )(after, sel, weights)


def quarter_of(me, flip, size):
    return pl.ds(pl.multiple_of((me ^ flip) * size, size), size)


def load_kernel(after, wg, wu, wd, vg, vu, vd, sem):
    rows = wg.shape[0] // 4
    copies = []
    for i in range(4):
        part = (pl.ds(i * rows, rows), slice(None))
        cols = (slice(None), pl.ds(i * rows, rows))
        copies.append(fetch(wg.at[part], vg.at[part], sem.at[0, i]))
        copies.append(fetch(wu.at[part], vu.at[part], sem.at[1, i]))
        copies.append(fetch(wd.at[cols], vd.at[cols], sem.at[2, i]))
    for copy in copies:
        copy.wait()


def load(after, *weights):
    return call(
        load_kernel,
        "load",
        tuple(array(w.shape) for w in weights),
        [aspec()] + [hspec()] * 3,
        vspec(),
        [pltpu.SemaphoreType.DMA((3, 4))],
        mib=4,
    )(after, *(fixed(w) for w in weights))


def pass_kernel(after, x, *outs):
    count = outs[0].shape[0]
    for n, out in enumerate(outs):
        out[...] = x[n * count : (n + 1) * count]


def pass_on(after, x, pieces):
    shape = (x.shape[0] // pieces, *x.shape[1:])
    out_shape = (array(shape),) * pieces
    return call(pass_kernel, "pass_on", out_shape, [aspec(), vspec()], vspec(), mib=4)(after, x)


def rows_of(first, rest, which):
    size = first.shape[3]
    return jnp.concatenate(
        [first[:, which].reshape(-1, size), rest[...].reshape(-1, size)], axis=0
    )


def forward_kernel(after, after_too, *refs):
    firsts, rests = refs[:4], refs[4:8]
    vg, vu, vd, act, lin, hidden, send, keep_far, keep_own = refs[8:]
    me = lax.axis_index("tp")
    size = firsts[0].shape[3]
    a = b = None
    for i in range(4):
        part = quarter_of(me, i, size)
        x = rows_of(firsts[i], rests[i], 0)
        pa = dot(x, vg[part, :])
        pb = dot(x, vu[part, :])
        a = pa if a is None else a + pa
        b = pb if b is None else b + pb
    act[...] = a
    lin[...] = b
    h = (a * jax.nn.sigmoid(a) * b).astype(BF16)
    hidden[...] = h
    for i, out in ((3, send.at[0]), (1, send.at[1]), (2, keep_far), (0, keep_own)):
        out[...] = dot(h, vd[:, quarter_of(me, i, size)]).astype(out.dtype)


def forward(after, after_too, firsts, rests, vg, vu, vd):
    size = firsts[0].shape[3]
    rows = (firsts[0].shape[0] + rests[0].shape[0]) * CAP
    ff = vg.shape[1]
    return call(
        forward_kernel,
        "forward",
        (array((rows, ff), F32),) * 2
        + (array((rows, ff)),)
        + (array((2, rows, size)),)
        + (array((rows, size), F32),) * 2,
        [aspec()] * 2 + [vspec()] * 11,
        vspec(),
    )(after, after_too, *firsts, *rests, vg, vu, vd)


def hidden_grad_kernel(*refs):
    firsts, rests = refs[:4], refs[4:8]
    act, lin, hidden, vd, dact, dlin, dots = refs[8:]
    me = lax.axis_index("tp")
    size = firsts[0].shape[3]
    rows = act.shape[0]
    dhid = None
    for i in range(4):
        p = dot(rows_of(firsts[i], rests[i], 1), vd[:, quarter_of(me, i, size)], NT)
        dhid = p if dhid is None else dhid + p
    a = act[...]
    s = jax.nn.sigmoid(a)
    dlin[...] = (dhid * (a * s)).astype(BF16)
    dact[...] = (dhid * lin[...] * s * (1.0 + a * (1.0 - s))).astype(BF16)
    per_row = jnp.sum(dhid * hidden[...].astype(F32), axis=1, keepdims=True)
    dots[...] = jnp.broadcast_to(per_row, (rows, LANES)).T[:8]


def hidden_grad(firsts, rests, act, lin, hidden, vd):
    rows, ff = act.shape
    return call(
        hidden_grad_kernel,
        "hidden_grad",
        (array((rows, ff)),) * 2 + (array((8, rows), F32),),
        [vspec()] * 12,
        vspec(),
    )(*firsts, *rests, act, lin, hidden, vd)


def pack_dots(dots, size):
    wide = jnp.concatenate([dots, jnp.zeros((8, size - dots.shape[1]), F32)], axis=1)
    high = wide.astype(BF16).astype(F32)
    top = lax.broadcasted_iota(jnp.int32, wide.shape, 0) == 0
    block = jnp.where(top, high, wide - high)
    return jnp.concatenate([block, block], axis=0).astype(BF16)


def unpack_dots(block, rows):
    block = block.astype(F32)
    return jnp.broadcast_to(block[0:1, :rows] + block[1:2, :rows], (8, rows))


def input_grad_kernel(flips, after, dots, dact, dlin, vg, vu, send, keep):
    me = lax.axis_index("tp")
    rows, size = keep.shape
    da = dact[...]
    dl = dlin[...]
    for i, out in zip(flips, (send, keep)):
        part = quarter_of(me, i, size)
        p = dot(da, vg[part, :], NT) + dot(dl, vu[part, :], NT)
        out[:rows] = p.astype(out.dtype)
    if send.shape[0] > rows:
        send[rows:] = pack_dots(dots[...], size)


def input_grad(flips, after, dots, dact, dlin, vg, vu, more=0):
    rows = dact.shape[0]
    size = vg.shape[0] // 4
    return call(
        functools.partial(input_grad_kernel, flips),
        "input_grad",
        (array((rows + more, size)), array((rows, size), F32)),
        [aspec()] + [vspec()] * 5,
        vspec(),
    )(after, dots, dact, dlin, vg, vu)


def half_kernel(places, after, o_keep, o_near, x_keep, x_near, dots, out):
    rows, size = o_keep.shape
    count = len(places) * CAP
    for n, p in enumerate(places):
        span = slice(p * CAP, (p + 1) * CAP)
        o = o_keep[span] + o_near[0, span].astype(F32)
        x = x_keep[span] + x_near[span].astype(F32)
        out[n * CAP : (n + 1) * CAP] = o.astype(BF16)
        out[count + n * CAP : count + (n + 1) * CAP] = x.astype(BF16)
    if out.shape[0] > 2 * count:
        out[2 * count :] = pack_dots(dots[...] + unpack_dots(x_near[rows:], rows), size)


def half(after, places, o_keep, o_near, x_keep, x_near, dots, more=0):
    size = o_keep.shape[1]
    return call(
        functools.partial(half_kernel, places),
        "half",
        array((2 * CAP * len(places) + more, size)),
        [aspec()] + [vspec()] * 5,
        vspec(),
    )(after, o_keep, o_near, x_keep, x_near, dots)


def grads_kernel(which, count, after, *refs):
    firsts, rests = refs[:4], refs[4:8]
    given = refs[8 : 8 + count]
    outs = refs[8 + count : 8 + 2 * count]
    made = refs[8 + 2 * count : 8 + 3 * count]
    sem = refs[8 + 3 * count]
    me = lax.axis_index("tp")
    size = firsts[0].shape[3]
    values = [g[...] for g in given]
    stores = []
    for i in range(4):
        part = quarter_of(me, i, size)
        rows = rows_of(firsts[i], rests[i], which)
        for n in range(count):
            if which == 0:
                at = (part, slice(None))
                made[n][at] = dot(rows, values[n], TN).astype(BF16)
            else:
                at = (slice(None), part)
                made[n][at] = dot(values[n], rows, TN).astype(BF16)
            stores.append(fetch(made[n].at[at], outs[n].at[at], sem.at[n, i]))
    for copy in stores:
        copy.wait()


def grads(after, which, firsts, rests, given):
    size = firsts[0].shape[3]
    rows, ff = given[0].shape
    count = len(given)
    shape = (4 * size, ff) if which == 0 else (ff, 4 * size)
    return call(
        functools.partial(grads_kernel, which, count),
        "grads",
        (array(shape),) * count,
        [aspec()] + [vspec()] * (8 + count),
        hspec(),
        [pltpu.VMEM(shape, BF16)] * count + [pltpu.SemaphoreType.DMA((count, 4))],
        mib=20,
        flops=2 * count * rows * ff * 4 * size,
        nbytes=2 * count * ff * 4 * size,
    )(after, *firsts, *rests, *given)


def total_kernel(places, after, o_keep, o_near, x_keep, x_near, far, dots, x_send, first, *outs):
    tiles, cap, lanes = outs[0].shape
    count = len(outs) * cap
    rows, size = o_keep.shape
    middle = tiles // 2
    d = dots[...] + unpack_dots(x_send[rows:], rows) + unpack_dots(first[first.shape[0] - 16 :], rows)
    d = jnp.broadcast_to(d[:1], (lanes, rows)).T
    high = d.astype(BF16).astype(F32)
    left = lax.broadcasted_iota(jnp.int32, (rows, lanes), 1) < lanes // 2
    d = jnp.where(left, high, d - high)
    for n, (p, out) in enumerate(zip(places, outs)):
        span = slice(p * cap, (p + 1) * cap)
        at = slice(n * cap, (n + 1) * cap)
        also = slice(count + n * cap, count + (n + 1) * cap)
        for j in range(middle):
            part = slice(j * lanes, (j + 1) * lanes)
            o = o_near[1, span, part].astype(F32) + far[at, part].astype(F32)
            out[j] = (o_keep[span, part] + o).astype(BF16)
            x = x_near[span, part].astype(F32) + far[also, part].astype(F32)
            out[middle + j] = (x_keep[span, part] + x).astype(BF16)
        out[tiles - 1] = d[span].astype(BF16)


def total(after, places, keeps, far, sums):
    size = far.shape[1]
    tiles = 2 * (size // LANES) + 1
    return call(
        functools.partial(total_kernel, places),
        "total",
        (array((tiles, CAP, LANES)),) * len(places),
        [aspec()] + [vspec()] * 8,
        vspec(),
    )(after, *keeps, far, *sums)


def combine_kernel(places, *refs):
    mix, pick, sel, routes, gates = refs[:5]
    back = [refs[5 + places.index(p)] for p in range(len(places))]
    mixed, d_tokens, d_gates, held_mixed, held_tokens, held_gates, sem = refs[5 + len(places) :]
    tiles, cap, lanes = back[0].shape
    slots, tok = sel.shape
    topk = routes.shape[0]
    experts = len(back)
    middle = tiles // 2
    span = middle // 2

    def columns(first):
        return jnp.concatenate(
            [jnp.concatenate([b[first + j] for j in range(span)], axis=1) for b in back], axis=0
        )

    copies = []
    for c in range(2):
        part = slice(c * span * lanes, (c + 1) * span * lanes)
        o = columns(c * span)
        both = jnp.concatenate([o, o], axis=0)
        held_mixed[:, part] = dot(mix[...], both).astype(BF16)
        copies.append(fetch(held_mixed.at[:, part], mixed.at[:, part], sem.at[0, c]))
        held_tokens[:, part] = dot(pick[...], columns(middle + c * span)).astype(BF16)
        copies.append(fetch(held_tokens.at[:, part], d_tokens.at[:, part], sem.at[1, c]))
        if c == 0:
            pair = jnp.concatenate([b[tiles - 1] for b in back], axis=0).astype(F32)
            per_slot = pair[:, :1] + pair[:, lanes // 2 : lanes // 2 + 1]
            spread = sel[...].astype(F32) * per_slot
            per_expert = jnp.sum(spread.reshape(experts, cap, tok), axis=1)
            match = routes[...][None] == relative(experts, topk, tok)
            scaled = jnp.sum(jnp.where(match, per_expert[:, None, :], 0.0), axis=0)
            held_gates[...] = scaled / gates[...]
            copies.append(fetch(held_gates, d_gates, sem.at[2, 0]))
    for copy in copies:
        copy.wait()


def combine(places, back, mix, pick, sel, routes_t, gates_t):
    quarter = back[0].shape[0] // 2 * LANES
    topk, tok = routes_t.shape
    return call(
        functools.partial(combine_kernel, places),
        "combine",
        (array((tok, quarter)), array((tok, quarter)), array((topk, tok), F32)),
        [vspec()] * (5 + len(back)),
        hspec(),
        [
            pltpu.VMEM((tok, quarter), BF16),
            pltpu.VMEM((tok, quarter), BF16),
            pltpu.VMEM((topk, tok), F32),
            pltpu.SemaphoreType.DMA((3, 2)),
        ],
    )(mix, pick, sel, routes_t, gates_t, *back)


def swap(x, flip):
    return lax.ppermute(x, "tp", [(i, i ^ flip) for i in range(4)])


def exchange(parts, places, count):
    assert count & (count - 1) == 0
    order = steps(count)
    return [
        lax.ppermute(part, "ctx", [(i, i ^ order[p]) for i in range(count)]) if p else part
        for part, p in zip(parts, places)
    ]


def on_device(tokens, routes, gates, w_gate, w_up, w_down, d_out):
    sources = lax.axis_size("ctx")
    routes_t, gates_t = routes.T, gates.T
    parts, (sel, weights) = dispatch(routes_t, gates_t, tokens, d_out, sources)
    got = exchange(parts, range(sources), sources)
    early = sources // 2
    cut = early * CAP
    rows = sources * CAP
    first = jnp.stack(got[:early])
    rest_x = jnp.stack([g[0] for g in got[early:]])
    rest_d = jnp.stack([g[1] for g in got[early:]])
    far_first = swap(first, 2)
    far_x = swap(rest_x, 2)
    far_d = swap(rest_d, 2)
    vg, vu, vd = load(first, w_gate[0], w_up[0], w_down[0])
    firsts = (first, swap(pass_on(vg, first, 1)[0], 1), far_first, swap(pass_on(vg, far_first, 1)[0], 1))
    xs = (rest_x, swap(rest_x, 1), far_x, swap(pass_on(vg, far_x, 1)[0], 1))
    ds = (rest_d, swap(rest_d, 1), far_d, swap(far_d, 1))

    act, lin, hidden, send, keep_far, keep_own = forward(ds[3], ds[1], firsts, xs, vg, vu, vd)
    near_out = swap(send, 1)
    dact, dlin, dots = hidden_grad(firsts, ds, act, lin, hidden, vd)
    send_dx, keep_dx = input_grad((3, 2), dots, dots, dact, dlin, vg, vu, more=16)
    near_send = swap(send_dx, 1)
    send_dx_near, keep_dx_own = input_grad((1, 0), send_dx, dots, dact, dlin, vg, vu)
    one, two, three = groups(sources)
    halves = (keep_far, near_out, keep_dx, near_send, dots)
    half_one = half(keep_dx_own, one, *halves, more=16)
    half_two = half(half_one, two, *halves)
    near_dx = swap(send_dx_near, 1)
    grad_gate, grad_up = grads(half_one, 0, firsts, xs, (dact, dlin))
    half_three = half(fixed(grad_gate), three, *halves)
    pick, mix = turn(vg, sel, weights)
    far_one, far_two, far_three = swap(half_one, 2), swap(half_two, 2), swap(half_three, 2)
    (grad_down,) = grads(half_one, 1, firsts, ds, (hidden,))
    keeps = (keep_own, near_out, keep_dx_own, near_dx)
    sums = (dots, near_send, far_one)
    back_one = total(fixed(grad_up), one, keeps, far_one, sums)
    back_two = total(back_one[0], two, keeps, far_two, sums)
    back_three = total(back_two[0], three, keeps, far_three, sums)
    places = [*one, *two, *three]
    back = exchange([*back_one, *back_two, *back_three], places, sources)
    mixed, d_tokens, d_gates = combine(places, back, mix, pick, sel, routes_t, gates_t)
    return (mixed, d_tokens, d_gates.T, grad_gate[None], grad_up[None], grad_down[None])


def solution(mesh):
    placed = (
        P("ctx", "tp"),
        P("ctx", None),
        P("ctx", None),
        P("ctx", None, "tp"),
        P("ctx", None, "tp"),
        P("ctx", "tp", None),
        P("ctx", "tp"),
    )
    return jax.shard_map(
        on_device,
        mesh=mesh,
        in_specs=placed,
        out_specs=(
            P("ctx", "tp"),
            P("ctx", "tp"),
            P("ctx", None),
            P("ctx", None, "tp"),
            P("ctx", None, "tp"),
            P("ctx", "tp", None),
        ),
        check_vma=False,
    )
```

```python
import functools

import jax
import jax.numpy as jnp
from jax import lax
from jax.experimental import pallas as pl
from jax.experimental.pallas import tpu as pltpu
from jax.sharding import PartitionSpec as P

CAP = 16
LANES = 128
F32 = jnp.float32
BF16 = jnp.bfloat16
NN = (((1,), (0,)), ((), ()))
NT = (((1,), (1,)), ((), ()))
TN = (((0,), (0,)), ((), ()))


def dot(a, b, dims=NN):
    return lax.dot_general(a, b, dims, preferred_element_type=F32)


def vspec():
    return pl.BlockSpec(memory_space=pltpu.VMEM)


def hspec():
    return pl.BlockSpec(memory_space=pltpu.HBM)


def aspec():
    return pl.BlockSpec(memory_space=pl.ANY)


def fixed(x):
    return pltpu.with_memory_space_constraint(x, pltpu.HBM)


def array(shape, dtype=BF16):
    return jax.ShapeDtypeStruct(shape, dtype)


def call(kernel, name, out_shape, in_specs, out_spec, scratch=(), mib=16, flops=0, nbytes=0):
    out_specs = (out_spec,) * len(out_shape) if isinstance(out_shape, tuple) else out_spec
    return pl.pallas_call(
        kernel,
        out_shape=out_shape,
        in_specs=in_specs,
        out_specs=out_specs,
        scratch_shapes=list(scratch),
        compiler_params=pltpu.CompilerParams(vmem_limit_bytes=mib * 1024 * 1024),
        cost_estimate=pl.CostEstimate(flops=flops, bytes_accessed=nbytes, transcendentals=0),
        name=name,
    )


def fetch(src, dst, sem):
    copy = pltpu.make_async_copy(src, dst, sem)
    copy.start()
    return copy


def steps(count):
    return [0] + sorted(range(1, count), key=lambda s: ([2, 6, 7, 1, 3, 4, 5].index(s) if count == 8 else -s))


def groups(count):
    if count == 8:
        listed = [[7, 6], [3, 5, 4], [2, 1, 0]]
    else:
        far = sorted(range(1, count), reverse=True) + [0]
        third = -(-count // 3)
        listed = [far[:third], far[third : 2 * third], far[2 * third :]]
    order = steps(count)
    return [[order.index(s) for s in group] for group in listed]


def relative(experts, topk, tok):
    place = lax.broadcasted_iota(jnp.int32, (experts, topk, tok), 0)
    distance = jnp.zeros_like(place)
    for p, s in enumerate(steps(experts)):
        distance = jnp.where(place == p, s, distance)
    return distance ^ lax.axis_index("ctx")


def dispatch_kernel(experts, *refs):
    routes_in, gates_in, tokens_in, d_in = refs[:4]
    outs = refs[4 : 4 + experts]
    sel, weights, routes, gates, tokens, d_out, sem = refs[4 + experts :]
    topk, tok = routes.shape
    slots = experts * CAP
    pairs = ((routes_in, routes), (gates_in, gates), (tokens_in, tokens), (d_in, d_out))
    loads = [fetch(src, dst, sem.at[i]) for i, (src, dst) in enumerate(pairs)]
    loads[0].wait()
    loads[1].wait()
    match = routes[...][None] == relative(experts, topk, tok)
    hit = jnp.sum(jnp.where(match, 1.0, 0.0), axis=1)
    gate = jnp.sum(jnp.where(match, gates[...][None], 0.0), axis=1)
    earlier = lax.broadcasted_iota(jnp.int32, (tok, tok), 0) < lax.broadcasted_iota(
        jnp.int32, (tok, tok), 1
    )
    before = dot(hit.astype(BF16), jnp.where(earlier, 1.0, 0.0).astype(BF16))
    place = jnp.where(hit > 0.0, before, -1.0)[:, None, :]
    row = lax.broadcasted_iota(jnp.int32, (experts, CAP, tok), 1).astype(F32)
    chosen = jnp.where(place == row, 1.0, 0.0)
    weight = (chosen * gate[:, None, :]).reshape(slots, tok)
    chosen = chosen.reshape(slots, tok)
    select = chosen.astype(BF16)
    loads[2].wait()
    x = dot(select, tokens[...]).astype(BF16)
    slot_gate = jnp.sum(weight, axis=1, keepdims=True)
    loads[3].wait()
    d = (slot_gate * dot(select, d_out[...])).astype(BF16)
    for e, out in enumerate(outs):
        out[0] = x[e * CAP : (e + 1) * CAP]
        out[1] = d[e * CAP : (e + 1) * CAP]
    sel[...] = select
    weights[...] = weight


def dispatch(routes_t, gates_t, tokens, d_out, experts):
    tok, quarter = tokens.shape
    slots = experts * CAP
    results = call(
        functools.partial(dispatch_kernel, experts),
        "dispatch",
        (array((2, CAP, quarter)),) * experts
        + (array((slots, tok)), array((slots, tok), F32)),
        [hspec()] * 4,
        vspec(),
        [
            pltpu.VMEM(routes_t.shape, jnp.int32),
            pltpu.VMEM(gates_t.shape, F32),
            pltpu.VMEM(tokens.shape, BF16),
            pltpu.VMEM(d_out.shape, BF16),
            pltpu.SemaphoreType.DMA((4,)),
        ],
    )(*(fixed(v) for v in (routes_t, gates_t, tokens, d_out)))
    return results[:experts], results[experts:]


def turn_kernel(after, sel, weights, pick, mix):
    slots = sel.shape[0]
    pick[...] = sel[...].astype(F32).T.astype(BF16)
    back = weights[...].T
    high = back.astype(BF16)
    mix[:, :slots] = high
    mix[:, slots:] = (back - high.astype(F32)).astype(BF16)


def turn(after, sel, weights):
    slots, tok = sel.shape
    return call(
        turn_kernel,
        "turn",
        (array((tok, slots)), array((tok, 2 * slots))),
        [aspec()] + [vspec()] * 2,
        vspec(),
    )(after, sel, weights)


def quarter_of(me, flip, size):
    return pl.ds(pl.multiple_of((me ^ flip) * size, size), size)


def load_kernel(after, wg, wu, wd, vg, vu, vd, sem):
    rows = wg.shape[0] // 4
    copies = []
    for i in range(4):
        part = (pl.ds(i * rows, rows), slice(None))
        cols = (slice(None), pl.ds(i * rows, rows))
        copies.append(fetch(wg.at[part], vg.at[part], sem.at[0, i]))
        copies.append(fetch(wu.at[part], vu.at[part], sem.at[1, i]))
        copies.append(fetch(wd.at[cols], vd.at[cols], sem.at[2, i]))
    for copy in copies:
        copy.wait()


def load(after, *weights):
    return call(
        load_kernel,
        "load",
        tuple(array(w.shape) for w in weights),
        [aspec()] + [hspec()] * 3,
        vspec(),
        [pltpu.SemaphoreType.DMA((3, 4))],
        mib=4,
    )(after, *(fixed(w) for w in weights))


def pass_kernel(after, x, *outs):
    count = outs[0].shape[0]
    for n, out in enumerate(outs):
        out[...] = x[n * count : (n + 1) * count]


def pass_on(after, x, pieces):
    shape = (x.shape[0] // pieces, *x.shape[1:])
    out_shape = (array(shape),) * pieces
    return call(pass_kernel, "pass_on", out_shape, [aspec(), vspec()], vspec(), mib=4)(after, x)


def rows_of(first, rest, which):
    size = first.shape[3]
    return jnp.concatenate(
        [first[:, which].reshape(-1, size), rest[...].reshape(-1, size)], axis=0
    )


def forward_kernel(after, after_too, *refs):
    firsts, rests = refs[:4], refs[4:8]
    vg, vu, vd, act, lin, hidden, send, keep_far, keep_own = refs[8:]
    me = lax.axis_index("tp")
    size = firsts[0].shape[3]
    a = b = None
    for i in range(4):
        part = quarter_of(me, i, size)
        x = rows_of(firsts[i], rests[i], 0)
        pa = dot(x, vg[part, :])
        pb = dot(x, vu[part, :])
        a = pa if a is None else a + pa
        b = pb if b is None else b + pb
    act[...] = a
    lin[...] = b
    h = (a * jax.nn.sigmoid(a) * b).astype(BF16)
    hidden[...] = h
    for i, out in ((3, send.at[0]), (1, send.at[1]), (2, keep_far), (0, keep_own)):
        out[...] = dot(h, vd[:, quarter_of(me, i, size)]).astype(out.dtype)


def forward(after, after_too, firsts, rests, vg, vu, vd):
    size = firsts[0].shape[3]
    rows = (firsts[0].shape[0] + rests[0].shape[0]) * CAP
    ff = vg.shape[1]
    return call(
        forward_kernel,
        "forward",
        (array((rows, ff), F32),) * 2
        + (array((rows, ff)),)
        + (array((2, rows, size)),)
        + (array((rows, size), F32),) * 2,
        [aspec()] * 2 + [vspec()] * 11,
        vspec(),
    )(after, after_too, *firsts, *rests, vg, vu, vd)


def hidden_grad_kernel(*refs):
    firsts, rests = refs[:4], refs[4:8]
    act, lin, hidden, vd, dact, dlin, dots = refs[8:]
    me = lax.axis_index("tp")
    size = firsts[0].shape[3]
    rows = act.shape[0]
    dhid = None
    for i in range(4):
        p = dot(rows_of(firsts[i], rests[i], 1), vd[:, quarter_of(me, i, size)], NT)
        dhid = p if dhid is None else dhid + p
    a = act[...]
    s = jax.nn.sigmoid(a)
    dlin[...] = (dhid * (a * s)).astype(BF16)
    dact[...] = (dhid * lin[...] * s * (1.0 + a * (1.0 - s))).astype(BF16)
    per_row = jnp.sum(dhid * hidden[...].astype(F32), axis=1, keepdims=True)
    dots[...] = jnp.broadcast_to(per_row, (rows, LANES)).T[:8]


def hidden_grad(firsts, rests, act, lin, hidden, vd):
    rows, ff = act.shape
    return call(
        hidden_grad_kernel,
        "hidden_grad",
        (array((rows, ff)),) * 2 + (array((8, rows), F32),),
        [vspec()] * 12,
        vspec(),
    )(*firsts, *rests, act, lin, hidden, vd)


def pack_dots(dots, size):
    wide = jnp.concatenate([dots, jnp.zeros((8, size - dots.shape[1]), F32)], axis=1)
    high = wide.astype(BF16).astype(F32)
    top = lax.broadcasted_iota(jnp.int32, wide.shape, 0) == 0
    block = jnp.where(top, high, wide - high)
    return jnp.concatenate([block, block], axis=0).astype(BF16)


def unpack_dots(block, rows):
    block = block.astype(F32)
    return jnp.broadcast_to(block[0:1, :rows] + block[1:2, :rows], (8, rows))


def input_grad_kernel(flips, after, dots, dact, dlin, vg, vu, send, keep):
    me = lax.axis_index("tp")
    rows, size = keep.shape
    da = dact[...]
    dl = dlin[...]
    for i, out in zip(flips, (send, keep)):
        part = quarter_of(me, i, size)
        p = dot(da, vg[part, :], NT) + dot(dl, vu[part, :], NT)
        out[:rows] = p.astype(out.dtype)
    if send.shape[0] > rows:
        send[rows:] = pack_dots(dots[...], size)


def input_grad(flips, after, dots, dact, dlin, vg, vu, more=0):
    rows = dact.shape[0]
    size = vg.shape[0] // 4
    return call(
        functools.partial(input_grad_kernel, flips),
        "input_grad",
        (array((rows + more, size)), array((rows, size), F32)),
        [aspec()] + [vspec()] * 5,
        vspec(),
    )(after, dots, dact, dlin, vg, vu)


def half_kernel(places, after, o_keep, o_near, x_keep, x_near, dots, out):
    rows, size = o_keep.shape
    count = len(places) * CAP
    for n, p in enumerate(places):
        span = slice(p * CAP, (p + 1) * CAP)
        o = o_keep[span] + o_near[0, span].astype(F32)
        x = x_keep[span] + x_near[span].astype(F32)
        out[n * CAP : (n + 1) * CAP] = o.astype(BF16)
        out[count + n * CAP : count + (n + 1) * CAP] = x.astype(BF16)
    if out.shape[0] > 2 * count:
        out[2 * count :] = pack_dots(dots[...] + unpack_dots(x_near[rows:], rows), size)


def half(after, places, o_keep, o_near, x_keep, x_near, dots, more=0):
    size = o_keep.shape[1]
    return call(
        functools.partial(half_kernel, places),
        "half",
        array((2 * CAP * len(places) + more, size)),
        [aspec()] + [vspec()] * 5,
        vspec(),
    )(after, o_keep, o_near, x_keep, x_near, dots)


def grads_kernel(which, count, after, *refs):
    firsts, rests = refs[:4], refs[4:8]
    given = refs[8 : 8 + count]
    outs = refs[8 + count : 8 + 2 * count]
    made = refs[8 + 2 * count : 8 + 3 * count]
    sem = refs[8 + 3 * count]
    me = lax.axis_index("tp")
    size = firsts[0].shape[3]
    values = [g[...] for g in given]
    stores = []
    for i in range(4):
        part = quarter_of(me, i, size)
        rows = rows_of(firsts[i], rests[i], which)
        for n in range(count):
            if which == 0:
                at = (part, slice(None))
                made[n][at] = dot(rows, values[n], TN).astype(BF16)
            else:
                at = (slice(None), part)
                made[n][at] = dot(values[n], rows, TN).astype(BF16)
            stores.append(fetch(made[n].at[at], outs[n].at[at], sem.at[n, i]))
    for copy in stores:
        copy.wait()


def grads(after, which, firsts, rests, given):
    size = firsts[0].shape[3]
    rows, ff = given[0].shape
    count = len(given)
    shape = (4 * size, ff) if which == 0 else (ff, 4 * size)
    return call(
        functools.partial(grads_kernel, which, count),
        "grads",
        (array(shape),) * count,
        [aspec()] + [vspec()] * (8 + count),
        hspec(),
        [pltpu.VMEM(shape, BF16)] * count + [pltpu.SemaphoreType.DMA((count, 4))],
        mib=20,
        flops=2 * count * rows * ff * 4 * size,
        nbytes=2 * count * ff * 4 * size,
    )(after, *firsts, *rests, *given)


def total_kernel(places, after, o_keep, o_near, x_keep, x_near, far, dots, x_send, first, *outs):
    tiles, cap, lanes = outs[0].shape
    count = len(outs) * cap
    rows, size = o_keep.shape
    middle = tiles // 2
    d = dots[...] + unpack_dots(x_send[rows:], rows) + unpack_dots(first[first.shape[0] - 16 :], rows)
    d = jnp.broadcast_to(d[:1], (lanes, rows)).T
    high = d.astype(BF16).astype(F32)
    left = lax.broadcasted_iota(jnp.int32, (rows, lanes), 1) < lanes // 2
    d = jnp.where(left, high, d - high)
    for n, (p, out) in enumerate(zip(places, outs)):
        span = slice(p * cap, (p + 1) * cap)
        at = slice(n * cap, (n + 1) * cap)
        also = slice(count + n * cap, count + (n + 1) * cap)
        for j in range(middle):
            part = slice(j * lanes, (j + 1) * lanes)
            o = o_near[1, span, part].astype(F32) + far[at, part].astype(F32)
            out[j] = (o_keep[span, part] + o).astype(BF16)
            x = x_near[span, part].astype(F32) + far[also, part].astype(F32)
            out[middle + j] = (x_keep[span, part] + x).astype(BF16)
        out[tiles - 1] = d[span].astype(BF16)


def total(after, places, keeps, far, sums):
    size = far.shape[1]
    tiles = 2 * (size // LANES) + 1
    return call(
        functools.partial(total_kernel, places),
        "total",
        (array((tiles, CAP, LANES)),) * len(places),
        [aspec()] + [vspec()] * 8,
        vspec(),
    )(after, *keeps, far, *sums)


def combine_kernel(places, *refs):
    mix, pick, sel, routes, gates = refs[:5]
    back = [refs[5 + places.index(p)] for p in range(len(places))]
    mixed, d_tokens, d_gates, held_mixed, held_tokens, held_gates, sem = refs[5 + len(places) :]
    tiles, cap, lanes = back[0].shape
    slots, tok = sel.shape
    topk = routes.shape[0]
    experts = len(back)
    middle = tiles // 2
    span = middle // 2

    def columns(first):
        return jnp.concatenate(
            [jnp.concatenate([b[first + j] for j in range(span)], axis=1) for b in back], axis=0
        )

    copies = []
    for c in range(2):
        part = slice(c * span * lanes, (c + 1) * span * lanes)
        o = columns(c * span)
        both = jnp.concatenate([o, o], axis=0)
        held_mixed[:, part] = dot(mix[...], both).astype(BF16)
        copies.append(fetch(held_mixed.at[:, part], mixed.at[:, part], sem.at[0, c]))
        held_tokens[:, part] = dot(pick[...], columns(middle + c * span)).astype(BF16)
        copies.append(fetch(held_tokens.at[:, part], d_tokens.at[:, part], sem.at[1, c]))
        if c == 0:
            pair = jnp.concatenate([b[tiles - 1] for b in back], axis=0).astype(F32)
            per_slot = pair[:, :1] + pair[:, lanes // 2 : lanes // 2 + 1]
            spread = sel[...].astype(F32) * per_slot
            per_expert = jnp.sum(spread.reshape(experts, cap, tok), axis=1)
            match = routes[...][None] == relative(experts, topk, tok)
            scaled = jnp.sum(jnp.where(match, per_expert[:, None, :], 0.0), axis=0)
            held_gates[...] = scaled / gates[...]
            copies.append(fetch(held_gates, d_gates, sem.at[2, 0]))
    for copy in copies:
        copy.wait()


def combine(places, back, mix, pick, sel, routes_t, gates_t):
    quarter = back[0].shape[0] // 2 * LANES
    topk, tok = routes_t.shape
    return call(
        functools.partial(combine_kernel, places),
        "combine",
        (array((tok, quarter)), array((tok, quarter)), array((topk, tok), F32)),
        [vspec()] * (5 + len(back)),
        hspec(),
        [
            pltpu.VMEM((tok, quarter), BF16),
            pltpu.VMEM((tok, quarter), BF16),
            pltpu.VMEM((topk, tok), F32),
            pltpu.SemaphoreType.DMA((3, 2)),
        ],
    )(mix, pick, sel, routes_t, gates_t, *back)


def swap(x, flip):
    return lax.ppermute(x, "tp", [(i, i ^ flip) for i in range(4)])


def exchange(parts, places, count):
    assert count & (count - 1) == 0
    order = steps(count)
    return [
        lax.ppermute(part, "ctx", [(i, i ^ order[p]) for i in range(count)]) if p else part
        for part, p in zip(parts, places)
    ]


def on_device(tokens, routes, gates, w_gate, w_up, w_down, d_out):
    sources = lax.axis_size("ctx")
    routes_t, gates_t = routes.T, gates.T
    parts, (sel, weights) = dispatch(routes_t, gates_t, tokens, d_out, sources)
    got = exchange(parts, range(sources), sources)
    early = sources // 2
    cut = early * CAP
    rows = sources * CAP
    first = jnp.stack(got[:early])
    rest_x = jnp.stack([g[0] for g in got[early:]])
    rest_d = jnp.stack([g[1] for g in got[early:]])
    far_first = swap(first, 2)
    far_x = swap(rest_x, 2)
    far_d = swap(rest_d, 2)
    vg, vu, vd = load(first, w_gate[0], w_up[0], w_down[0])
    firsts = (first, swap(pass_on(vg, first, 1)[0], 1), far_first, swap(far_first, 1))
    xs = (rest_x, swap(rest_x, 1), far_x, swap(pass_on(vg, far_x, 1)[0], 1))
    ds = (rest_d, swap(rest_d, 1), far_d, swap(far_d, 1))

    act, lin, hidden, send, keep_far, keep_own = forward(ds[3], ds[1], firsts, xs, vg, vu, vd)
    near_out = swap(send, 1)
    dact, dlin, dots = hidden_grad(firsts, ds, act, lin, hidden, vd)
    send_dx, keep_dx = input_grad((3, 2), dots, dots, dact, dlin, vg, vu, more=16)
    near_send = swap(send_dx, 1)
    send_dx_near, keep_dx_own = input_grad((1, 0), send_dx, dots, dact, dlin, vg, vu)
    one, two, three = groups(sources)
    halves = (keep_far, near_out, keep_dx, near_send, dots)
    half_one = half(keep_dx_own, one, *halves, more=16)
    half_two = half(half_one, two, *halves)
    near_dx = swap(send_dx_near, 1)
    grad_gate, grad_up = grads(half_one, 0, firsts, xs, (dact, dlin))
    half_three = half(fixed(grad_gate), three, *halves)
    pick, mix = turn(vg, sel, weights)
    far_one, far_two, far_three = swap(half_one, 2), swap(half_two, 2), swap(half_three, 2)
    (grad_down,) = grads(half_one, 1, firsts, ds, (hidden,))
    keeps = (keep_own, near_out, keep_dx_own, near_dx)
    sums = (dots, near_send, far_one)
    back_one = total(fixed(grad_up), one, keeps, far_one, sums)
    back_two = total(back_one[0], two, keeps, far_two, sums)
    back_three = total(back_two[0], three, keeps, far_three, sums)
    places = [*one, *two, *three]
    back = exchange([*back_one, *back_two, *back_three], places, sources)
    mixed, d_tokens, d_gates = combine(places, back, mix, pick, sel, routes_t, gates_t)
    return (mixed, d_tokens, d_gates.T, grad_gate[None], grad_up[None], grad_down[None])


def solution(mesh):
    placed = (
        P("ctx", "tp"),
        P("ctx", None),
        P("ctx", None),
        P("ctx", None, "tp"),
        P("ctx", None, "tp"),
        P("ctx", "tp", None),
        P("ctx", "tp"),
    )
    return jax.shard_map(
        on_device,
        mesh=mesh,
        in_specs=placed,
        out_specs=(
            P("ctx", "tp"),
            P("ctx", "tp"),
            P("ctx", None),
            P("ctx", None, "tp"),
            P("ctx", None, "tp"),
            P("ctx", "tp", None),
        ),
        check_vma=False,
    )
```

```python
import functools

import jax
import jax.numpy as jnp
from jax import lax
from jax.experimental import pallas as pl
from jax.experimental.pallas import tpu as pltpu
from jax.sharding import PartitionSpec as P

CAP = 16
LANES = 128
F32 = jnp.float32
BF16 = jnp.bfloat16
NN = (((1,), (0,)), ((), ()))
NT = (((1,), (1,)), ((), ()))
TN = (((0,), (0,)), ((), ()))


def dot(a, b, dims=NN):
    return lax.dot_general(a, b, dims, preferred_element_type=F32)


def vspec():
    return pl.BlockSpec(memory_space=pltpu.VMEM)


def hspec():
    return pl.BlockSpec(memory_space=pltpu.HBM)


def aspec():
    return pl.BlockSpec(memory_space=pl.ANY)


def fixed(x):
    return pltpu.with_memory_space_constraint(x, pltpu.HBM)


def array(shape, dtype=BF16):
    return jax.ShapeDtypeStruct(shape, dtype)


def call(kernel, name, out_shape, in_specs, out_spec, scratch=(), mib=16, flops=0, nbytes=0):
    out_specs = (out_spec,) * len(out_shape) if isinstance(out_shape, tuple) else out_spec
    return pl.pallas_call(
        kernel,
        out_shape=out_shape,
        in_specs=in_specs,
        out_specs=out_specs,
        scratch_shapes=list(scratch),
        compiler_params=pltpu.CompilerParams(vmem_limit_bytes=mib * 1024 * 1024),
        cost_estimate=pl.CostEstimate(flops=flops, bytes_accessed=nbytes, transcendentals=0),
        name=name,
    )


def fetch(src, dst, sem):
    copy = pltpu.make_async_copy(src, dst, sem)
    copy.start()
    return copy


def steps(count):
    return [0] + sorted(range(1, count), key=lambda s: ([2, 6, 7, 1, 3, 4, 5].index(s) if count == 8 else -s))


def groups(count):
    if count == 8:
        listed = [[7, 6], [3, 5, 4], [2, 1, 0]]
    else:
        far = sorted(range(1, count), reverse=True) + [0]
        third = -(-count // 3)
        listed = [far[:third], far[third : 2 * third], far[2 * third :]]
    order = steps(count)
    return [[order.index(s) for s in group] for group in listed]


def relative(experts, topk, tok):
    place = lax.broadcasted_iota(jnp.int32, (experts, topk, tok), 0)
    distance = jnp.zeros_like(place)
    for p, s in enumerate(steps(experts)):
        distance = jnp.where(place == p, s, distance)
    return distance ^ lax.axis_index("ctx")


def dispatch_kernel(experts, *refs):
    routes_in, gates_in, tokens_in, d_in = refs[:4]
    outs = refs[4 : 4 + experts]
    sel, weights, routes, gates, tokens, d_out, sem = refs[4 + experts :]
    topk, tok = routes.shape
    slots = experts * CAP
    pairs = ((routes_in, routes), (gates_in, gates), (tokens_in, tokens), (d_in, d_out))
    loads = [fetch(src, dst, sem.at[i]) for i, (src, dst) in enumerate(pairs)]
    loads[0].wait()
    loads[1].wait()
    match = routes[...][None] == relative(experts, topk, tok)
    hit = jnp.sum(jnp.where(match, 1.0, 0.0), axis=1)
    gate = jnp.sum(jnp.where(match, gates[...][None], 0.0), axis=1)
    earlier = lax.broadcasted_iota(jnp.int32, (tok, tok), 0) < lax.broadcasted_iota(
        jnp.int32, (tok, tok), 1
    )
    before = dot(hit.astype(BF16), jnp.where(earlier, 1.0, 0.0).astype(BF16))
    place = jnp.where(hit > 0.0, before, -1.0)[:, None, :]
    row = lax.broadcasted_iota(jnp.int32, (experts, CAP, tok), 1).astype(F32)
    chosen = jnp.where(place == row, 1.0, 0.0)
    weight = (chosen * gate[:, None, :]).reshape(slots, tok)
    chosen = chosen.reshape(slots, tok)
    select = chosen.astype(BF16)
    loads[2].wait()
    x = dot(select, tokens[...]).astype(BF16)
    slot_gate = jnp.sum(weight, axis=1, keepdims=True)
    loads[3].wait()
    d = (slot_gate * dot(select, d_out[...])).astype(BF16)
    for e, out in enumerate(outs):
        out[0] = x[e * CAP : (e + 1) * CAP]
        out[1] = d[e * CAP : (e + 1) * CAP]
    sel[...] = select
    weights[...] = weight


def dispatch(routes_t, gates_t, tokens, d_out, experts):
    tok, quarter = tokens.shape
    slots = experts * CAP
    results = call(
        functools.partial(dispatch_kernel, experts),
        "dispatch",
        (array((2, CAP, quarter)),) * experts
        + (array((slots, tok)), array((slots, tok), F32)),
        [hspec()] * 4,
        vspec(),
        [
            pltpu.VMEM(routes_t.shape, jnp.int32),
            pltpu.VMEM(gates_t.shape, F32),
            pltpu.VMEM(tokens.shape, BF16),
            pltpu.VMEM(d_out.shape, BF16),
            pltpu.SemaphoreType.DMA((4,)),
        ],
    )(*(fixed(v) for v in (routes_t, gates_t, tokens, d_out)))
    return results[:experts], results[experts:]


def turn_kernel(after, sel, weights, pick, mix):
    slots = sel.shape[0]
    pick[...] = sel[...].astype(F32).T.astype(BF16)
    back = weights[...].T
    high = back.astype(BF16)
    mix[:, :slots] = high
    mix[:, slots:] = (back - high.astype(F32)).astype(BF16)


def turn(after, sel, weights):
    slots, tok = sel.shape
    return call(
        turn_kernel,
        "turn",
        (array((tok, slots)), array((tok, 2 * slots))),
        [aspec()] + [vspec()] * 2,
        vspec(),
    )(after, sel, weights)


def quarter_of(me, flip, size):
    return pl.ds(pl.multiple_of((me ^ flip) * size, size), size)


def load_kernel(after, wg, wu, wd, vg, vu, vd, sem):
    rows = wg.shape[0] // 4
    copies = []
    for i in range(4):
        part = (pl.ds(i * rows, rows), slice(None))
        cols = (slice(None), pl.ds(i * rows, rows))
        copies.append(fetch(wg.at[part], vg.at[part], sem.at[0, i]))
        copies.append(fetch(wu.at[part], vu.at[part], sem.at[1, i]))
        copies.append(fetch(wd.at[cols], vd.at[cols], sem.at[2, i]))
    for copy in copies:
        copy.wait()


def load(after, *weights):
    return call(
        load_kernel,
        "load",
        tuple(array(w.shape) for w in weights),
        [aspec()] + [hspec()] * 3,
        vspec(),
        [pltpu.SemaphoreType.DMA((3, 4))],
        mib=4,
    )(after, *(fixed(w) for w in weights))


def pass_kernel(after, x, *outs):
    count = outs[0].shape[0]
    for n, out in enumerate(outs):
        out[...] = x[n * count : (n + 1) * count]


def pass_on(after, x, pieces):
    shape = (x.shape[0] // pieces, *x.shape[1:])
    out_shape = (array(shape),) * pieces
    return call(pass_kernel, "pass_on", out_shape, [aspec(), vspec()], vspec(), mib=4)(after, x)


def rows_of(first, rest, which):
    size = first.shape[3]
    return jnp.concatenate(
        [first[:, which].reshape(-1, size), rest[...].reshape(-1, size)], axis=0
    )


def forward_kernel(after, after_too, *refs):
    firsts, rests = refs[:4], refs[4:8]
    vg, vu, vd, act, lin, hidden, send, keep_far, keep_own = refs[8:]
    me = lax.axis_index("tp")
    size = firsts[0].shape[3]
    a = b = None
    for i in range(4):
        part = quarter_of(me, i, size)
        x = rows_of(firsts[i], rests[i], 0)
        pa = dot(x, vg[part, :])
        pb = dot(x, vu[part, :])
        a = pa if a is None else a + pa
        b = pb if b is None else b + pb
    act[...] = a
    lin[...] = b
    h = (a * jax.nn.sigmoid(a) * b).astype(BF16)
    hidden[...] = h
    for i, out in ((3, send.at[0]), (1, send.at[1]), (2, keep_far), (0, keep_own)):
        out[...] = dot(h, vd[:, quarter_of(me, i, size)]).astype(out.dtype)


def forward(after, after_too, firsts, rests, vg, vu, vd):
    size = firsts[0].shape[3]
    rows = (firsts[0].shape[0] + rests[0].shape[0]) * CAP
    ff = vg.shape[1]
    return call(
        forward_kernel,
        "forward",
        (array((rows, ff), F32),) * 2
        + (array((rows, ff)),)
        + (array((2, rows, size)),)
        + (array((rows, size), F32),) * 2,
        [aspec()] * 2 + [vspec()] * 11,
        vspec(),
    )(after, after_too, *firsts, *rests, vg, vu, vd)


def hidden_grad_kernel(*refs):
    firsts, rests = refs[:4], refs[4:8]
    act, lin, hidden, vd, dact, dlin, dots = refs[8:]
    me = lax.axis_index("tp")
    size = firsts[0].shape[3]
    rows = act.shape[0]
    dhid = None
    for i in range(4):
        p = dot(rows_of(firsts[i], rests[i], 1), vd[:, quarter_of(me, i, size)], NT)
        dhid = p if dhid is None else dhid + p
    a = act[...]
    s = jax.nn.sigmoid(a)
    dlin[...] = (dhid * (a * s)).astype(BF16)
    dact[...] = (dhid * lin[...] * s * (1.0 + a * (1.0 - s))).astype(BF16)
    per_row = jnp.sum(dhid * hidden[...].astype(F32), axis=1, keepdims=True)
    dots[...] = jnp.broadcast_to(per_row, (rows, LANES)).T[:8]


def hidden_grad(firsts, rests, act, lin, hidden, vd):
    rows, ff = act.shape
    return call(
        hidden_grad_kernel,
        "hidden_grad",
        (array((rows, ff)),) * 2 + (array((8, rows), F32),),
        [vspec()] * 12,
        vspec(),
    )(*firsts, *rests, act, lin, hidden, vd)


def pack_dots(dots, size):
    wide = jnp.concatenate([dots, jnp.zeros((8, size - dots.shape[1]), F32)], axis=1)
    high = wide.astype(BF16).astype(F32)
    top = lax.broadcasted_iota(jnp.int32, wide.shape, 0) == 0
    block = jnp.where(top, high, wide - high)
    return jnp.concatenate([block, block], axis=0).astype(BF16)


def unpack_dots(block, rows):
    block = block.astype(F32)
    return jnp.broadcast_to(block[0:1, :rows] + block[1:2, :rows], (8, rows))


def input_grad_kernel(flips, after, dots, dact, dlin, vg, vu, send, keep):
    me = lax.axis_index("tp")
    rows, size = keep.shape
    da = dact[...]
    dl = dlin[...]
    for i, out in zip(flips, (send, keep)):
        part = quarter_of(me, i, size)
        p = dot(da, vg[part, :], NT) + dot(dl, vu[part, :], NT)
        out[:rows] = p.astype(out.dtype)
    if send.shape[0] > rows:
        send[rows:] = pack_dots(dots[...], size)


def input_grad(flips, after, dots, dact, dlin, vg, vu, more=0):
    rows = dact.shape[0]
    size = vg.shape[0] // 4
    return call(
        functools.partial(input_grad_kernel, flips),
        "input_grad",
        (array((rows + more, size)), array((rows, size), F32)),
        [aspec()] + [vspec()] * 5,
        vspec(),
    )(after, dots, dact, dlin, vg, vu)


def half_kernel(places, after, o_keep, o_near, x_keep, x_near, dots, out):
    rows, size = o_keep.shape
    count = len(places) * CAP
    for n, p in enumerate(places):
        span = slice(p * CAP, (p + 1) * CAP)
        o = o_keep[span] + o_near[0, span].astype(F32)
        x = x_keep[span] + x_near[span].astype(F32)
        out[n * CAP : (n + 1) * CAP] = o.astype(BF16)
        out[count + n * CAP : count + (n + 1) * CAP] = x.astype(BF16)
    if out.shape[0] > 2 * count:
        out[2 * count :] = pack_dots(dots[...] + unpack_dots(x_near[rows:], rows), size)


def half(after, places, o_keep, o_near, x_keep, x_near, dots, more=0):
    size = o_keep.shape[1]
    return call(
        functools.partial(half_kernel, places),
        "half",
        array((2 * CAP * len(places) + more, size)),
        [aspec()] + [vspec()] * 5,
        vspec(),
    )(after, o_keep, o_near, x_keep, x_near, dots)


def grads_kernel(which, count, after, *refs):
    firsts, rests = refs[:4], refs[4:8]
    given = refs[8 : 8 + count]
    outs = refs[8 + count : 8 + 2 * count]
    made = refs[8 + 2 * count : 8 + 3 * count]
    sem = refs[8 + 3 * count]
    me = lax.axis_index("tp")
    size = firsts[0].shape[3]
    values = [g[...].T if which else g[...] for g in given]
    piece = size // 2
    stores = []
    for i in range(4):
        rows = rows_of(firsts[i], rests[i], which)
        for j in range(2):
            part = pl.ds(pl.multiple_of((me ^ i) * size + j * piece, piece), piece)
            some = rows[:, j * piece : (j + 1) * piece]
            for n in range(count):
                if which == 0:
                    at = (part, slice(None))
                    made[n][at] = dot(some, values[n], TN).astype(BF16)
                else:
                    at = (slice(None), part)
                    made[n][at] = dot(values[n], some).astype(BF16)
                stores.append(fetch(made[n].at[at], outs[n].at[at], sem.at[n, 2 * i + j]))
    for copy in stores:
        copy.wait()


def grads(after, which, firsts, rests, given):
    size = firsts[0].shape[3]
    rows, ff = given[0].shape
    count = len(given)
    shape = (4 * size, ff) if which == 0 else (ff, 4 * size)
    return call(
        functools.partial(grads_kernel, which, count),
        "grads",
        (array(shape),) * count,
        [aspec()] + [vspec()] * (8 + count),
        hspec(),
        [pltpu.VMEM(shape, BF16)] * count + [pltpu.SemaphoreType.DMA((count, 8))],
        mib=20,
        flops=2 * count * rows * ff * 4 * size,
        nbytes=2 * count * ff * 4 * size,
    )(after, *firsts, *rests, *given)


def total_kernel(places, after, o_keep, o_near, x_keep, x_near, far, dots, x_send, first, *outs):
    tiles, cap, lanes = outs[0].shape
    count = len(outs) * cap
    rows, size = o_keep.shape
    middle = tiles // 2
    d = dots[...] + unpack_dots(x_send[rows:], rows) + unpack_dots(first[first.shape[0] - 16 :], rows)
    d = jnp.broadcast_to(d[:1], (lanes, rows)).T
    high = d.astype(BF16).astype(F32)
    left = lax.broadcasted_iota(jnp.int32, (rows, lanes), 1) < lanes // 2
    d = jnp.where(left, high, d - high)
    for n, (p, out) in enumerate(zip(places, outs)):
        span = slice(p * cap, (p + 1) * cap)
        at = slice(n * cap, (n + 1) * cap)
        also = slice(count + n * cap, count + (n + 1) * cap)
        for j in range(middle):
            part = slice(j * lanes, (j + 1) * lanes)
            o = o_near[1, span, part].astype(F32) + far[at, part].astype(F32)
            out[j] = (o_keep[span, part] + o).astype(BF16)
            x = x_near[span, part].astype(F32) + far[also, part].astype(F32)
            out[middle + j] = (x_keep[span, part] + x).astype(BF16)
        out[tiles - 1] = d[span].astype(BF16)


def total(after, places, keeps, far, sums):
    size = far.shape[1]
    tiles = 2 * (size // LANES) + 1
    return call(
        functools.partial(total_kernel, places),
        "total",
        (array((tiles, CAP, LANES)),) * len(places),
        [aspec()] + [vspec()] * 8,
        vspec(),
    )(after, *keeps, far, *sums)


def combine_kernel(places, *refs):
    mix, pick, sel, routes, gates = refs[:5]
    back = [refs[5 + places.index(p)] for p in range(len(places))]
    mixed, d_tokens, d_gates, held_mixed, held_tokens, held_gates, sem = refs[5 + len(places) :]
    tiles, cap, lanes = back[0].shape
    slots, tok = sel.shape
    topk = routes.shape[0]
    experts = len(back)
    middle = tiles // 2
    span = middle // 2

    def columns(first):
        return jnp.concatenate(
            [jnp.concatenate([b[first + j] for j in range(span)], axis=1) for b in back], axis=0
        )

    copies = []
    for c in range(2):
        part = slice(c * span * lanes, (c + 1) * span * lanes)
        o = columns(c * span)
        both = jnp.concatenate([o, o], axis=0)
        held_mixed[:, part] = dot(mix[...], both).astype(BF16)
        copies.append(fetch(held_mixed.at[:, part], mixed.at[:, part], sem.at[0, c]))
        held_tokens[:, part] = dot(pick[...], columns(middle + c * span)).astype(BF16)
        copies.append(fetch(held_tokens.at[:, part], d_tokens.at[:, part], sem.at[1, c]))
        if c == 0:
            pair = jnp.concatenate([b[tiles - 1] for b in back], axis=0).astype(F32)
            per_slot = pair[:, :1] + pair[:, lanes // 2 : lanes // 2 + 1]
            spread = sel[...].astype(F32) * per_slot
            per_expert = jnp.sum(spread.reshape(experts, cap, tok), axis=1)
            match = routes[...][None] == relative(experts, topk, tok)
            scaled = jnp.sum(jnp.where(match, per_expert[:, None, :], 0.0), axis=0)
            held_gates[...] = scaled / gates[...]
            copies.append(fetch(held_gates, d_gates, sem.at[2, 0]))
    for copy in copies:
        copy.wait()


def combine(places, back, mix, pick, sel, routes_t, gates_t):
    quarter = back[0].shape[0] // 2 * LANES
    topk, tok = routes_t.shape
    return call(
        functools.partial(combine_kernel, places),
        "combine",
        (array((tok, quarter)), array((tok, quarter)), array((topk, tok), F32)),
        [vspec()] * (5 + len(back)),
        hspec(),
        [
            pltpu.VMEM((tok, quarter), BF16),
            pltpu.VMEM((tok, quarter), BF16),
            pltpu.VMEM((topk, tok), F32),
            pltpu.SemaphoreType.DMA((3, 2)),
        ],
    )(mix, pick, sel, routes_t, gates_t, *back)


def swap(x, flip):
    return lax.ppermute(x, "tp", [(i, i ^ flip) for i in range(4)])


def exchange(parts, places, count):
    assert count & (count - 1) == 0
    order = steps(count)
    return [
        lax.ppermute(part, "ctx", [(i, i ^ order[p]) for i in range(count)]) if p else part
        for part, p in zip(parts, places)
    ]


def on_device(tokens, routes, gates, w_gate, w_up, w_down, d_out):
    sources = lax.axis_size("ctx")
    routes_t, gates_t = routes.T, gates.T
    parts, (sel, weights) = dispatch(routes_t, gates_t, tokens, d_out, sources)
    got = exchange(parts, range(sources), sources)
    early = sources // 2
    cut = early * CAP
    rows = sources * CAP
    first = jnp.stack(got[:early])
    rest_x = jnp.stack([g[0] for g in got[early:]])
    rest_d = jnp.stack([g[1] for g in got[early:]])
    far_first = swap(first, 2)
    far_x = swap(rest_x, 2)
    far_d = swap(rest_d, 2)
    vg, vu, vd = load(first, w_gate[0], w_up[0], w_down[0])
    firsts = (first, swap(pass_on(vg, first, 1)[0], 1), far_first, swap(far_first, 1))
    xs = (rest_x, swap(rest_x, 1), far_x, swap(pass_on(vg, far_x, 1)[0], 1))
    ds = (rest_d, swap(rest_d, 1), far_d, swap(far_d, 1))

    act, lin, hidden, send, keep_far, keep_own = forward(ds[3], ds[1], firsts, xs, vg, vu, vd)
    near_out = swap(send, 1)
    dact, dlin, dots = hidden_grad(firsts, ds, act, lin, hidden, vd)
    send_dx, keep_dx = input_grad((3, 2), dots, dots, dact, dlin, vg, vu, more=16)
    near_send = swap(send_dx, 1)
    send_dx_near, keep_dx_own = input_grad((1, 0), send_dx, dots, dact, dlin, vg, vu)
    one, two, three = groups(sources)
    halves = (keep_far, near_out, keep_dx, near_send, dots)
    half_one = half(keep_dx_own, one, *halves, more=16)
    half_two = half(half_one, two, *halves)
    near_dx = swap(send_dx_near, 1)
    grad_gate, grad_up = grads(half_one, 0, firsts, xs, (dact, dlin))
    half_three = half(fixed(grad_gate), three, *halves)
    pick, mix = turn(vg, sel, weights)
    far_one, far_two, far_three = swap(half_one, 2), swap(half_two, 2), swap(half_three, 2)
    (grad_down,) = grads(half_one, 1, firsts, ds, (hidden,))
    keeps = (keep_own, near_out, keep_dx_own, near_dx)
    sums = (dots, near_send, far_one)
    back_one = total(fixed(grad_up), one, keeps, far_one, sums)
    back_two = total(back_one[0], two, keeps, far_two, sums)
    back_three = total(back_two[0], three, keeps, far_three, sums)
    places = [*one, *two, *three]
    back = exchange([*back_one, *back_two, *back_three], places, sources)
    mixed, d_tokens, d_gates = combine(places, back, mix, pick, sel, routes_t, gates_t)
    return (mixed, d_tokens, d_gates.T, grad_gate[None], grad_up[None], grad_down[None])


def solution(mesh):
    placed = (
        P("ctx", "tp"),
        P("ctx", None),
        P("ctx", None),
        P("ctx", None, "tp"),
        P("ctx", None, "tp"),
        P("ctx", "tp", None),
        P("ctx", "tp"),
    )
    return jax.shard_map(
        on_device,
        mesh=mesh,
        in_specs=placed,
        out_specs=(
            P("ctx", "tp"),
            P("ctx", "tp"),
            P("ctx", None),
            P("ctx", None, "tp"),
            P("ctx", None, "tp"),
            P("ctx", "tp", None),
        ),
        check_vma=False,
    )
```
